128 devices in a mesh: tm: 16 (over z_hi, y, core), space: 8 (over z_lo, x).
Axes of the slice: x: 4, y: 4, z: 4 (z_hi: 2, z_lo: 2; z = z_hi * 2 + z_lo), core: 2. Of those that a mesh axis runs over, the one named last changes fastest.
Arguments:
- forcing: float32 [16, 8, 512, 1024], P('tm', 'space'), may hold values from -6 to 6
- iterate: float32 [16, 8, 512, 1024], P('tm', 'space'), may hold values from -6 to 6
- forward_state: float32 [16, 8, 512, 1024], P('tm', 'space'), may hold values from -6 to 6
- conductivity: float32 [8, 512, 1024], P('space'), may hold values from 0.5 to 2
- terminal: float32 [8, 512, 1024], P('space'), may hold values from -6 to 6
Outputs:
- renewed: float32 [16, 8, 512, 1024], P('tm', 'space')
- gradient: float32 [8, 512, 1024], P('space', 'tm')
The draws below stay inside these ranges and needn't reach their ends.
All inputs are finite; a program needn't handle non-finite values.
Results may differ from the reference program's by a relative error of at most 0.0003.
Values sent between devices are 32-bit elements; how exact they have to be, the bound alone decides.
A program may use at most 128 MiB of HBM per device.

```python
import math
import jax
import jax.numpy as jnp
from jax import lax

NX = 1024
NY = 512
NT = 16
NZ = 8


def level_of(own_key, extent, split, least, largest):
    loudness, own = 1.0, jax.random.fold_in(own_key, 6)
    for position, blocks in split:
        heights = jnp.exp(jax.random.uniform(jax.random.fold_in(own, position), (blocks,), jnp.float32, least / len(split), largest / len(split)))
        loudness = loudness * jnp.repeat(heights, extent[position] // blocks).reshape([-1 if axis == position else 1 for axis in range(len(extent))])
    return loudness


def noise(own_key, extent, width, bound, cuts=(), kind=jnp.bfloat16):
    result = width * jax.random.normal(own_key, extent, jnp.float32)
    if cuts:
        result = result * level_of(own_key, extent, cuts, -0.22, 0.18)
    return jnp.clip(result, -bound, bound).astype(kind)


def setup_inputs(seed: int = 0) -> dict:
    key_list = jax.random.split(jax.random.key(seed), 6)
    return {
        "forcing": noise(key_list[0], (NT, NZ, NY, NX), 1.0, 6.0, ((0, 16), (1, 8)), jnp.float32),
        "iterate": noise(key_list[1], (NT, NZ, NY, NX), 1.0, 6.0, ((0, 16), (1, 8)), jnp.float32),
        "forward_state": noise(key_list[2], (NT, NZ, NY, NX), 1.0, 6.0, ((0, 16), (1, 8)), jnp.float32),
        "conductivity": jnp.clip(jnp.exp(math.log(2.0) - 1.3862944 * jax.random.uniform(key_list[3], (NZ, NY, NX), jnp.float32) ** level_of(key_list[3], (NZ, NY, NX), ((0, 8),), -0.2, 0.2)), 0.5, 2.0),
        "terminal": noise(key_list[4], (NZ, NY, NX), 1.0, 6.0, ((0, 8),), jnp.float32),
    }


inv_dt = 4.0
wrap_alpha = 0.25
kappa_ref = 1.0
highest = lax.Precision.HIGHEST

def along(field, kappa, axis):
    length = kappa.shape[axis]
    kaxis = kappa.ndim + axis
    face = 0.5 * (lax.slice_in_dim(kappa, 1, length, axis=kaxis) + lax.slice_in_dim(kappa, 0, length - 1, axis=kaxis))
    flux = face * jnp.diff(field, axis=axis)
    lower = [(0, 0)] * field.ndim
    upper = [(0, 0)] * field.ndim
    lower[field.ndim + axis] = (1, 0)
    upper[field.ndim + axis] = (0, 1)
    return jnp.pad(flux, lower) - jnp.pad(flux, upper)

def faces_sum(product, axis):
    lower = [(0, 0)] * product.ndim
    upper = [(0, 0)] * product.ndim
    lower[product.ndim + axis] = (1, 0)
    upper[product.ndim + axis] = (0, 1)
    return jnp.pad(product, lower) + jnp.pad(product, upper)

def cosine_table(length):
    rows_j = jnp.arange(length, dtype=jnp.int32)[:, None]
    cols_c = jnp.arange(length, dtype=jnp.int32)[None, :]
    angle = math.pi * (rows_j * (2 * cols_c + 1) % (4 * length)).astype(jnp.float32) / (2 * length)
    factor = jnp.where(rows_j == 0, math.sqrt(1.0 / length), math.sqrt(2.0 / length)).astype(jnp.float32)
    return factor * jnp.cos(angle)

def eigen(length):
    index = jnp.arange(length, dtype=jnp.int32).astype(jnp.float32)
    return 2.0 - 2.0 * jnp.cos(math.pi * index / length)

def reference(forcing, iterate, forward_state, conductivity, terminal):
    total_steps = forcing.shape[0]
    layers, rows, cols = conductivity.shape
    applied = along(iterate, conductivity, -1) + along(iterate, conductivity, -2) + along(iterate, conductivity, -3)
    earlier = jnp.concatenate([terminal[None], iterate[:-1]], axis=0)
    resid = forcing - (inv_dt * (iterate - earlier) + applied)
    steps_f = jnp.arange(total_steps, dtype=jnp.int32).astype(jnp.float32)
    scale = jnp.power(jnp.asarray(wrap_alpha, jnp.float32), steps_f / total_steps)
    modes = jnp.fft.ifft(scale[:, None, None, None] * resid, axis=0)
    tab_z = cosine_table(layers)
    tab_y = cosine_table(rows)
    tab_x = cosine_table(cols)
    mu_all = eigen(layers)[:, None, None] + eigen(rows)[:, None] + eigen(cols)
    root = wrap_alpha ** (1.0 / total_steps)

    def forward3(field):
        field = jnp.einsum('iyx,ji->jyx', field, tab_z, precision=highest)
        field = jnp.einsum('ziq,ji->zjq', field, tab_y, precision=highest)
        return jnp.einsum('zyi,ji->zyj', field, tab_x, precision=highest)

    def inverse3(field):
        field = jnp.einsum('jyx,ji->iyx', field, tab_z, precision=highest)
        field = jnp.einsum('zjq,ji->ziq', field, tab_y, precision=highest)
        return jnp.einsum('zyj,ji->zyi', field, tab_x, precision=highest)

    def solve_mode(inputs):
        part_re, part_im, mode = inputs
        hat_re = forward3(part_re)
        hat_im = forward3(part_im)
        theta = 2.0 * math.pi * mode.astype(jnp.float32) / total_steps
        real_den = (1.0 - root * jnp.cos(theta)) * inv_dt + kappa_ref * mu_all
        imag_den = -root * jnp.sin(theta) * inv_dt
        magnitude = real_den * real_den + imag_den * imag_den
        sol_re = (hat_re * real_den + hat_im * imag_den) / magnitude
        sol_im = (hat_im * real_den - hat_re * imag_den) / magnitude
        return (inverse3(sol_re), inverse3(sol_im))
    back_re, back_im = lax.map(solve_mode, (jnp.real(modes), jnp.imag(modes), jnp.arange(total_steps, dtype=jnp.int32)))
    combined = jnp.fft.fft(back_re + 1j * back_im, axis=0)
    update = jnp.real(combined) / scale[:, None, None, None]
    renewed = iterate + update
    total = 0.0
    for axis in (-1, -2, -3):
        product = lax.optimization_barrier(jnp.sum(0.5 * jnp.diff(renewed, axis=axis) * jnp.diff(forward_state, axis=axis), axis=0))
        total = total + faces_sum(product, axis)
    gradient = -total / total_steps
    return (renewed, gradient)
```

```python
import functools
import math

import jax
import jax.numpy as jnp
import numpy as np
from jax import lax
from jax.experimental import pallas as pl
from jax.experimental.pallas import tpu as pltpu
from jax.sharding import PartitionSpec as P

inv_dt = 4.0
wrap_alpha = 0.25
high = lax.Precision.HIGH
both = ("tm", "space")


def table(length):
    j = np.arange(length)[:, None]
    c = np.arange(length)[None, :]
    angle = math.pi * ((j * (2 * c + 1)) % (4 * length)) / (2 * length)
    factor = np.where(j == 0, math.sqrt(1.0 / length), math.sqrt(2.0 / length))
    return factor * np.cos(angle)


def device_table(length):
    j = jnp.arange(length, dtype=jnp.int32)[:, None]
    c = jnp.arange(length, dtype=jnp.int32)[None, :]
    angle = math.pi * (j * (2 * c + 1) % (4 * length)).astype(jnp.float32) / (2 * length)
    factor = jnp.where(j == 0, math.sqrt(1.0 / length), math.sqrt(2.0 / length)).astype(jnp.float32)
    return factor * jnp.cos(angle)


def eigen_at(index, length):
    return 2.0 - 2.0 * jnp.cos(math.pi * index.astype(jnp.float32) / length)


def solve_kernel(mu_ref, r_ref, out_ref):
    steps, layers = r_ref.shape[:2]
    tab = table(layers)
    lam = [2.0 - 2.0 * math.cos(math.pi * j / layers) for j in range(layers)]
    half = layers // 2
    mu = mu_ref[...]
    w = [1.0 / (inv_dt + lam[j] + mu) for j in range(layers)]
    q = [inv_dt * w[j] for j in range(layers)]
    state = [None] * layers
    for m in range(steps):
        v = [r_ref[m, z] for z in range(layers)]
        even = [v[z] + v[layers - 1 - z] for z in range(half)]
        odd = [v[z] - v[layers - 1 - z] for z in range(half)]
        for j in range(layers):
            src = even if j % 2 == 0 else odd
            acc = src[0] * float(tab[j, 0])
            for z in range(1, half):
                acc = acc + src[z] * float(tab[j, z])
            acc = acc * w[j]
            state[j] = acc if m == 0 else q[j] * state[j] + acc
            out_ref[m, j] = state[j]
    carry = []
    for j in range(layers):
        p = q[j]
        for _ in range(int(math.log2(steps))):
            p = p * p
        carry.append(wrap_alpha * state[j] / (1.0 - wrap_alpha * p))
    for m in range(steps):
        for j in range(layers):
            carry[j] = q[j] * carry[j]
        u = [out_ref[m, j] + carry[j] for j in range(layers)]
        for z in range(half):
            e = u[0] * float(tab[0, z])
            for j in range(2, layers, 2):
                e = e + u[j] * float(tab[j, z])
            o = u[1] * float(tab[1, z])
            for j in range(3, layers, 2):
                o = o + u[j] * float(tab[j, z])
            out_ref[m, z] = e + o
            out_ref[m, layers - 1 - z] = e - o


def solve(r, mu):
    steps, layers, rows, cols = r.shape
    lanes = 128
    return pl.pallas_call(
        solve_kernel,
        grid=(cols // lanes,),
        in_specs=[
            pl.BlockSpec((rows, lanes), lambda i: (0, i)),
            pl.BlockSpec((steps, layers, rows, lanes), lambda i: (0, 0, 0, i)),
        ],
        out_specs=pl.BlockSpec((steps, layers, rows, lanes), lambda i: (0, 0, 0, i)),
        out_shape=jax.ShapeDtypeStruct(r.shape, r.dtype),
        name="solve",
    )(mu, r)


def shift(x, axis, by):
    n = lax.axis_size(axis)
    return lax.ppermute(x, axis, [(i, i + by) for i in range(n) if 0 <= i + by < n])


def diff_pair(field, kappa, axis):
    n = field.shape[axis]
    hi = lambda a: lax.slice_in_dim(a, 1, n, axis=axis)
    lo = lambda a: lax.slice_in_dim(a, 0, n - 1, axis=axis)
    flux = 0.5 * (hi(kappa) + lo(kappa)) * (hi(field) - lo(field))
    pads = [(0, 0), (0, 0)]
    first, last = list(pads), list(pads)
    first[axis], last[axis] = (1, 0), (0, 1)
    return jnp.pad(flux, first) - jnp.pad(flux, last)


def face_products(a, b, axis):
    n = a.shape[axis]
    hi = lambda v: lax.slice_in_dim(v, 1, n, axis=axis)
    lo = lambda v: lax.slice_in_dim(v, 0, n - 1, axis=axis)
    product = 0.5 * (hi(a) - lo(a)) * (hi(b) - lo(b))
    pads = [(0, 0), (0, 0)]
    first, last = list(pads), list(pads)
    first[axis], last[axis] = (1, 0), (0, 1)
    return jnp.pad(product, first) + jnp.pad(product, last)


def body(forcing, iterate, forward_state, conductivity, terminal):
    rows, cols = iterate.shape[2:]
    steps, layers = lax.axis_size("tm"), lax.axis_size("space")
    half = cols // 2
    it, fo, fs = iterate[0, 0], forcing[0, 0], forward_state[0, 0]
    kappa, term = conductivity[0], terminal[0]
    tm, space = lax.axis_index("tm"), lax.axis_index("space")

    def chunks(plane):
        return plane.reshape(rows // 8, 8, 2, half).transpose(0, 2, 1, 3).reshape(-1, 8, half)

    state_c = lax.all_to_all(chunks(fs), both, 0, 0, tiled=True).reshape(steps, layers, 8, half)

    pair = jnp.stack([it, kappa])
    below, above = shift(pair, "space", 1), shift(pair, "space", -1)
    behind = shift(it, "tm", 1)
    has_below = (space > 0).astype(jnp.float32)
    has_above = (space < layers - 1).astype(jnp.float32)
    applied = (
        diff_pair(it, kappa, 1)
        + diff_pair(it, kappa, 0)
        + has_below * 0.5 * (kappa + below[1]) * (it - below[0])
        + has_above * 0.5 * (kappa + above[1]) * (it - above[0])
    )
    earlier = jnp.where(tm == 0, term, behind)
    resid = fo - (inv_dt * (it - earlier) + applied)

    tab_x, tab_y = device_table(cols), device_table(rows)
    hat_x = jnp.einsum("yi,ji->yj", resid, tab_x, precision=high)
    hat = jnp.stack(
        [jnp.einsum("iq,ji->jq", hat_x[:, h * half : (h + 1) * half], tab_y, precision=high) for h in range(2)]
    )
    gathered = lax.all_to_all(hat.reshape(-1, 8, half), both, 0, 0, tiled=True)
    chunk = tm * layers + space
    per = rows // 8
    row_index = (chunk % per) * 8 + jnp.arange(8, dtype=jnp.int32)
    col_index = (chunk // per) * half + jnp.arange(half, dtype=jnp.int32)
    mu = eigen_at(row_index, rows)[:, None] + eigen_at(col_index, cols)[None, :]
    solved = solve(gathered.reshape(steps, layers, 8, half), mu)
    back = lax.all_to_all(solved.reshape(-1, 8, half), both, 0, 0, tiled=True)
    back = back.reshape(2, rows, half)
    inv_y = jnp.einsum("hjq,ji->hiq", back, tab_y, precision=high)
    update = jnp.einsum("hyj,hji->yi", inv_y, tab_x.reshape(2, half, cols), precision=high)
    renewed = it + update

    renew_c = lax.all_to_all(chunks(renewed), both, 0, 0, tiled=True).reshape(steps, layers, 8, half)
    face = jnp.sum(
        0.5 * (renew_c[:, 1:] - renew_c[:, :-1]) * (state_c[:, 1:] - state_c[:, :-1]), axis=0
    )
    vertical = jnp.pad(face, ((1, 0), (0, 0), (0, 0))) + jnp.pad(face, ((0, 1), (0, 0), (0, 0)))
    vertical = lax.all_to_all(vertical, "space", 0, 0, tiled=True)
    vertical = vertical.reshape(layers // 2, 2, 8, half).transpose(0, 2, 1, 3).reshape(-1, cols)
    plane = face_products(renewed, fs, 1) + face_products(renewed, fs, 0)
    summed = lax.psum_scatter(plane, "tm", scatter_dimension=0, tiled=True)
    gradient = -(summed + vertical) / steps
    return renewed[None, None], gradient[None]


def solution(mesh):
    field, layer = P("tm", "space", None, None), P("space", None, None)
    return jax.shard_map(
        body,
        mesh=mesh,
        in_specs=(field, field, field, layer, layer),
        out_specs=(field, P("space", "tm", None)),
        check_vma=False,
    )
```

```python
import functools
import math

import jax
import jax.numpy as jnp
import ml_dtypes
import numpy as np
from jax import lax
from jax.experimental import pallas as pl
from jax.experimental.pallas import tpu as pltpu
from jax.sharding import PartitionSpec as P

inv_dt = 4.0
wrap_alpha = 0.25
MESH = pl.DeviceIdType.MESH
stride = 37
parts = 4
f32, bf16 = jnp.float32, jnp.bfloat16


def table(length):
    j = np.arange(length)[:, None]
    c = np.arange(length)[None, :]
    angle = math.pi * ((j * (2 * c + 1)) % (4 * length)) / (2 * length)
    factor = np.where(j == 0, math.sqrt(1.0 / length), math.sqrt(2.0 / length))
    return factor * np.cos(angle)


def eigen(length):
    return 2.0 - 2.0 * np.cos(math.pi * np.arange(length) / length)


def halves(tab):
    hi = tab.astype(ml_dtypes.bfloat16)
    lo = (tab - hi.astype(np.float64)).astype(ml_dtypes.bfloat16)
    return np.stack([hi, lo])


def split(x):
    hi = x.astype(bf16)
    return hi, (x - hi.astype(f32)).astype(bf16)


def dot3(ah, al, bh, bl):
    d = lambda a, b: jnp.dot(a, b, preferred_element_type=f32)
    return d(ah, bh) + d(ah, bl) + d(al, bh)


def take(ref, sem):
    pltpu.make_async_copy(ref, ref, sem).wait()


def kernel(rows, cols, steps, layers,
           it_h, fo_h, fs_h, ka_h, te_h, qx_h, qxt_h, qy_h, qyt_h, ey_h, ex_h,
           rn_h, gr_h,
           itv, kav, fov, fsv, below, above, kbelow, kabove, prev,
           qx, qxt, qy, qyt, ey, ex,
           rh, rl, xh, xl, hat, spec, back, bh, bl, yh, yl, upd, fsc, rnc,
           face, edge, edges, tot, got, grad,
           local, halo_s, halo_r, prev_s, prev_r, k1s, k1r, k2s, k2r, k3s, k3r,
           fwd_s, fwd_r, bck_s, bck_r, fs_s, fs_r, rn_s, rn_r, ed_s, ed_r, gz_s, gz_r):
    tm, s = lax.axis_index("tm"), lax.axis_index("space")
    count = steps * layers
    me = tm * layers + s
    half, quarter = cols // 2, cols // 4
    part = rows // parts
    core, ypos, zhi = lax.rem(tm, 2), lax.rem(lax.div(tm, 2), 4), lax.div(tm, 8)

    def remote(src, dst, send, recv, to):
        return pltpu.make_async_remote_copy(src, dst, send, recv, device_id=to, device_id_type=MESH)

    def coords(d):
        return (lax.div(d, layers), lax.rem(d, layers))

    def sent(ref, sem):
        remote(ref, ref, sem, sem, (lax.rem(tm + 1, steps), s)).wait_send()

    body_it = itv.at[pl.ds(8, rows)]
    body_ka = kav.at[pl.ds(8, rows)]
    loads = [(it_h, body_it), (ka_h, body_ka), (fo_h, fov), (qxt_h, qxt), (qy_h, qy),
             (ey_h, ey), (ex_h, ex), (fs_h, fsv), (qx_h, qx), (qyt_h, qyt)]
    copies = [pltpu.make_async_copy(a, b, local.at[i]) for i, (a, b) in enumerate(loads)]
    for c in copies:
        c.start()

    barrier = pltpu.get_barrier_semaphore()

    def greet(i, c):
        pl.semaphore_signal(barrier, 1, device_id=coords(lax.rem(me + i, count)), device_id_type=MESH)
        return c

    lax.fori_loop(1, count, greet, 0)
    pl.semaphore_wait(barrier, count - 1)

    width = rows // 8

    def krows(y, c):
        return pl.ds(pl.multiple_of((y * 2 + c) * width, 8), width)

    mine = krows(ypos, core)
    not_last, not_first = s < layers - 1, s > 0
    k_up = remote(ka_h.at[mine], kbelow.at[mine], k1s.at[0], k1r.at[0], (tm, jnp.minimum(s + 1, layers - 1)))
    k_dn = remote(ka_h.at[mine], kabove.at[mine], k1s.at[1], k1r.at[1], (tm, jnp.maximum(s - 1, 0)))

    @pl.when(not_last)
    def _():
        k_up.start()

    @pl.when(not_first)
    def _():
        k_dn.start()

    @pl.when(s == 0)
    def _():
        pltpu.make_async_copy(ka_h.at[mine], kbelow.at[mine], k1r.at[0]).start()

    @pl.when(s == layers - 1)
    def _():
        pltpu.make_async_copy(ka_h.at[mine], kabove.at[mine], k1r.at[1]).start()

    def prows(i):
        return pl.ds(pl.multiple_of(i * part, 8), part)

    def halo_start(i, c):
        r = prows(i)

        @pl.when(not_last)
        def _():
            remote(it_h.at[r], below.at[r], halo_s.at[0, i], halo_r.at[0, i], (tm, jnp.minimum(s + 1, layers - 1))).start()

        @pl.when(not_first)
        def _():
            remote(it_h.at[r], above.at[r], halo_s.at[1, i], halo_r.at[1, i], (tm, jnp.maximum(s - 1, 0))).start()

        @pl.when(tm < steps - 1)
        def _():
            remote(it_h.at[r], prev.at[r], prev_s.at[i], prev_r.at[i], (jnp.minimum(tm + 1, steps - 1), s)).start()

        @pl.when(s == 0)
        def _():
            pltpu.make_async_copy(it_h.at[r], below.at[r], halo_r.at[0, i]).start()

        @pl.when(s == layers - 1)
        def _():
            pltpu.make_async_copy(it_h.at[r], above.at[r], halo_r.at[1, i]).start()

        @pl.when(tm == 0)
        def _():
            pltpu.make_async_copy(te_h.at[r], prev.at[r], prev_r.at[i]).start()

        return c

    lax.fori_loop(0, parts, halo_start, 0)

    for i in range(3):
        copies[i].wait()

    lane = lax.broadcasted_iota(jnp.int32, (8, cols), 1)
    sub = lax.broadcasted_iota(jnp.int32, (8, cols), 0)

    def in_plane(b, c):
        r = pl.multiple_of(b * 8, 8)
        vs, ks = itv[pl.ds(r, 24), :], kav[pl.ds(r, 24), :]
        v, vu, vd = vs[8:16], vs[9:17], vs[7:15]
        k, ku, kd = ks[8:16], ks[9:17], ks[7:15]
        fx = 0.5 * (pltpu.roll(k, cols - 1, 1) + k) * (pltpu.roll(v, cols - 1, 1) - v)
        fx = jnp.where(lane == cols - 1, 0.0, fx)
        fu = jnp.where(sub + r == rows - 1, 0.0, 0.5 * (ku + k) * (vu - v))
        fd = jnp.where(sub + r == 0, 0.0, 0.5 * (k + kd) * (v - vd))
        applied = (pltpu.roll(fx, 1, 1) - fx) + (fd - fu)
        fov[pl.ds(r, 8), :] = fov[pl.ds(r, 8), :] - (inv_dt * v + applied)
        return c

    blocks = rows // 8
    lax.fori_loop(0, blocks // 4, in_plane, 0)
    take(kbelow.at[mine], k1r.at[0])
    take(kabove.at[mine], k1r.at[1])

    def along_y(i, c):
        to = (zhi * 8 + lax.rem(ypos + i, 4) * 2 + core, s)
        remote(kbelow.at[mine], kbelow.at[mine], k2s, k2r, to).start()
        remote(kabove.at[mine], kabove.at[mine], k2s, k2r, to).start()
        return c

    lax.fori_loop(1, 4, along_y, 0)
    lax.fori_loop(blocks // 4, blocks, in_plane, 0)
    take(kbelow.at[pl.ds(0, 6 * width)], k2r)

    def across(i, c):
        r = krows(i, core)
        to = (zhi * 8 + ypos * 2 + 1 - core, s)
        remote(kbelow.at[r], kbelow.at[r], k3s, k3r, to).start()
        remote(kabove.at[r], kabove.at[r], k3s, k3r, to).start()
        return c

    lax.fori_loop(0, 4, across, 0)
    take(kbelow, k3r)
    copies[3].wait()

    def fs_send(i, c):
        d = lax.rem(me + i * stride, count)
        src = fs_h.at[pl.ds(pl.multiple_of(lax.div(d, 2) * 8, 8), 8), pl.ds(pl.multiple_of(lax.rem(d, 2) * half, half), half)]
        remote(src, fsc.at[me], fs_s, fs_r, coords(d)).start()
        return c

    def arrive(i, c):
        r = prows(i)
        take(below.at[r], halo_r.at[0, i])
        take(above.at[r], halo_r.at[1, i])
        take(prev.at[r], prev_r.at[i])

        def resid(b, c):
            q = pl.multiple_of(i * part + b * 16, 16)
            at = lambda ref, off=0: ref[pl.ds(q + off, 16), :]
            v, k = at(itv, 8), at(kav, 8)
            x = at(fov) + inv_dt * at(prev)
            x = x - 0.5 * (k + at(kbelow)) * (v - at(below)) - 0.5 * (k + at(kabove)) * (v - at(above))
            hi, lo = split(x)
            o = pl.multiple_of(b * 16, 16)
            rh[pl.ds(o, 16), :] = hi
            rl[pl.ds(o, 16), :] = lo
            return c

        lax.fori_loop(0, part // 16, resid, 0)
        for n in range(4):
            cs = slice(n * quarter, (n + 1) * quarter)
            acc = dot3(rh[...], rl[...], qxt[0, :, cs], qxt[1, :, cs])
            hi, lo = split(acc)
            xh[pl.ds(pl.multiple_of(i * part, 16), part), cs] = hi
            xl[pl.ds(pl.multiple_of(i * part, 16), part), cs] = lo
        return c

    lax.fori_loop(0, parts, arrive, 0)
    copies[4].wait()

    my_rows = pl.ds(pl.multiple_of(lax.div(me, 2) * 8, 8), 8)

    def piece(d, p):
        return (pl.ds(pl.multiple_of(lax.div(d, 2) * 8, 8), 8),
                pl.ds(pl.multiple_of(p * half + lax.rem(d, 2) * quarter, quarter), quarter))

    for p in range(2):
        for n in range(2):
            cs = slice(p * half + n * quarter, p * half + (n + 1) * quarter)
            hat[:, cs] = dot3(qy[0], qy[1], xh[:, cs], xl[:, cs])

        def fwd(i, c, p=p):
            d = lax.rem(me + i * stride, count)
            remote(hat.at[piece(d, p)], spec.at[p, me], fwd_s.at[p], fwd_r.at[p], coords(d)).start()
            return c

        lax.fori_loop(1, count, fwd, 0)
        spec[p, me] = hat[piece(me, p)]

    lax.fori_loop(1, count, fs_send, 0)
    own_fs = pltpu.make_async_copy(fs_h.at[my_rows, pl.ds(pl.multiple_of(lax.rem(me, 2) * half, half), half)], fsc.at[me], local.at[10])
    own_fs.start()

    copies[5].wait()
    copies[6].wait()
    tab = table(layers)
    lam = eigen(layers)
    lz = layers // 2
    for p in range(2):
        take(spec.at[p, pl.ds(0, count - 1)], fwd_r.at[p])
        mu = ey[my_rows, :] + ex[:, pl.ds(pl.multiple_of(p * half + lax.rem(me, 2) * quarter, quarter), quarter)]
        w = [1.0 / (mu + (inv_dt + float(lam[j]))) for j in range(layers)]
        q = [inv_dt * w[j] for j in range(layers)]

        def forward(m, state, p=p, w=w, q=q):
            v = [spec[p, m * layers + z] for z in range(layers)]
            even = [v[z] + v[layers - 1 - z] for z in range(lz)]
            odd = [v[z] - v[layers - 1 - z] for z in range(lz)]
            new = []
            for j in range(layers):
                src = odd if j % 2 else even
                acc = src[0] * float(tab[j, 0])
                for z in range(1, lz):
                    acc = acc + src[z] * float(tab[j, z])
                u = q[j] * state[j] + w[j] * acc
                spec[p, m * layers + j] = u
                new.append(u)
            return tuple(new)

        state = lax.fori_loop(0, steps, forward, tuple(jnp.zeros((8, quarter), f32) for _ in range(layers)))
        carry = []
        for j in range(layers):
            t = q[j]
            for _ in range(int(math.log2(steps))):
                t = t * t
            carry.append(wrap_alpha * state[j] / (1.0 - wrap_alpha * t))

        def backward(m, carry, p=p, q=q):
            carry = tuple(q[j] * carry[j] for j in range(layers))
            u = [spec[p, m * layers + j] + carry[j] for j in range(layers)]
            for z in range(lz):
                e = u[0] * float(tab[0, z])
                o = u[1] * float(tab[1, z])
                for j in range(2, layers, 2):
                    e = e + u[j] * float(tab[j, z])
                    o = o + u[j + 1] * float(tab[j + 1, z])
                spec[p, m * layers + z] = e + o
                spec[p, m * layers + layers - 1 - z] = e - o
            return carry

        lax.fori_loop(0, steps, backward, tuple(carry))

        def bck(i, c, p=p):
            d = lax.rem(me + i * stride, count)
            remote(spec.at[p, d], back.at[piece(me, p)], bck_s.at[p], bck_r.at[p], coords(d)).start()
            return c

        lax.fori_loop(1, count, bck, 0)
        back[piece(me, p)] = spec[p, me]

    copies[8].wait()
    copies[9].wait()

    def to_plane(p):
        take(spec.at[p, pl.ds(0, count - 1)], bck_r.at[p])
        for n in range(2):
            cs = slice(p * half + n * quarter, p * half + (n + 1) * quarter)
            hi, lo = split(back[:, cs])
            acc = dot3(qyt[0], qyt[1], hi, lo)
            hi, lo = split(acc)
            yh[:, n * quarter:(n + 1) * quarter] = hi
            yl[:, n * quarter:(n + 1) * quarter] = lo

    def along_x(p, r, n):
        cs = slice(n * quarter, (n + 1) * quarter)
        ks = slice(p * half, (p + 1) * half)
        return dot3(yh[r, :], yl[r, :], qx[0, ks, cs], qx[1, ks, cs])

    to_plane(0)

    def first(i, c):
        r = pl.ds(pl.multiple_of(i * part, 16), part)
        for n in range(4):
            cs = slice(n * quarter, (n + 1) * quarter)
            upd[r, cs] = itv[pl.ds(pl.multiple_of(i * part, 16) + 8, part), cs] + along_x(0, r, n)
        return c

    lax.fori_loop(0, parts, first, 0)
    to_plane(1)
    per = count // parts

    def second(i, c):
        g = lax.rem(i + me, parts)
        start = pl.multiple_of(g * part, 16)
        r = pl.ds(start, part)
        for n in range(4):
            cs = slice(n * quarter, (n + 1) * quarter)
            upd[r, cs] = upd[r, cs] + along_x(1, r, n)

        def rn_send(j, c):
            d = g * per + lax.rem(me + j * 5, per)
            src = upd.at[pl.ds(pl.multiple_of(lax.div(d, 2) * 8, 8), 8), pl.ds(pl.multiple_of(lax.rem(d, 2) * half, half), half)]

            @pl.when(d != me)
            def _():
                remote(src, rnc.at[me], rn_s, rn_r, coords(d)).start()

            return c

        lax.fori_loop(0, per, rn_send, 0)
        pltpu.make_async_copy(upd.at[r], rn_h.at[r], local.at[11]).start()
        return c

    lax.fori_loop(0, parts, second, 0)
    rnc[me] = upd[my_rows, pl.ds(pl.multiple_of(lax.rem(me, 2) * half, half), half)]

    copies[7].wait()
    nb = rows // 8
    face[0:1, :] = jnp.zeros((1, cols), f32)
    face[pl.ds(nb, 8), :] = jnp.zeros((8, cols), f32)
    for f in range(1, nb):
        d_rn = upd[8 * f:8 * f + 1, :] - upd[8 * f - 1:8 * f, :]
        d_fs = fsv[8 * f:8 * f + 1, :] - fsv[8 * f - 1:8 * f, :]
        face[f:f + 1, :] = 0.5 * d_rn * d_fs
    tall = rows // steps
    eye = lax.broadcasted_iota(jnp.int32, (tall, 128), 0) == lax.broadcasted_iota(jnp.int32, (tall, 128), 1)
    row8 = lax.broadcasted_iota(jnp.int32, (8, cols), 0)

    for g in range(steps):
        r = slice(g * tall, (g + 1) * tall)
        d_rn = upd[r, half:half + 128] - pltpu.roll(upd[r, half - 128:half], 1, 1)
        d_fs = fsv[r, half:half + 128] - pltpu.roll(fsv[r, half - 128:half], 1, 1)
        px = 0.5 * d_rn * d_fs
        line = jnp.sum(jnp.where(eye, px[:, 0:1], 0.0), axis=0, keepdims=True)
        edge[g] = face[g * (tall // 8):g * (tall // 8) + 8, :]
        edge[g, 5:6, 0:128] = line

    def edge_send(i, c):
        g = lax.rem(tm + i, steps)
        remote(edge.at[g], edges.at[tm], ed_s, ed_r, (g, s)).start()
        return c

    lax.fori_loop(1, steps, edge_send, 0)
    edges[tm] = edge[tm]

    take(fsc.at[pl.ds(0, count - 1)], fs_r)
    own_fs.wait()
    take(rnc.at[pl.ds(0, count - 1)], rn_r)
    lane8 = lax.broadcasted_iota(jnp.int32, (8, half), 1)
    sub8 = lax.broadcasted_iota(jnp.int32, (8, half), 0)
    zero = jnp.zeros((8, half), f32)
    fz = zero
    for z in range(layers):

        def gather(t, c, z=z):
            fx, fy, fzz = c
            a, b = rnc[t * layers + z], fsc[t * layers + z]
            fx = fx + (pltpu.roll(a, half - 1, 1) - a) * (pltpu.roll(b, half - 1, 1) - b)
            fy = fy + (pltpu.roll(a, 7, 0) - a) * (pltpu.roll(b, 7, 0) - b)
            if z < layers - 1:
                fzz = fzz + (rnc[t * layers + z + 1] - a) * (fsc[t * layers + z + 1] - b)
            return fx, fy, fzz

        fx, fy, nz = lax.fori_loop(0, steps, gather, (zero, zero, zero))
        fx = jnp.where(lane8 == half - 1, 0.0, fx)
        fy = jnp.where(sub8 == 7, 0.0, fy)
        tot[z] = 0.5 * (fx + pltpu.roll(fx, 1, 1) + fy + pltpu.roll(fy, 1, 0) + fz + nz)
        fz = nz

    def tot_send(i, c):
        z = lax.rem(s + i, layers)
        remote(tot.at[z], got.at[s], gz_s, gz_r, (tm, z)).start()
        return c

    lax.fori_loop(1, layers, tot_send, 0)
    got[s] = tot[s]
    take(edges.at[pl.ds(0, steps - 1)], ed_r)
    total = edges[0]
    for t in range(1, steps):
        total = total + edges[t]
    face[0:8, :] = total
    column = jnp.sum(jnp.where(eye, face[5:6, 0:128], 0.0), axis=1, keepdims=True)
    take(got.at[pl.ds(0, layers - 1)], gz_r)
    for r in range(tall // 8):
        for h in range(2):
            cs = slice(h * half, (h + 1) * half)
            val = got[2 * r + h]
            val = val + jnp.where(sub8 == 0, face[r:r + 1, cs], 0.0)
            val = val + jnp.where(sub8 == 7, face[r + 1:r + 2, cs], 0.0)
            val = val + jnp.where(lane8 == (half - 1 if h == 0 else 0), column[8 * r:8 * r + 8], 0.0)
            grad[8 * r:8 * r + 8, cs] = val * (-1.0 / steps)
    out = pltpu.make_async_copy(grad, gr_h, local.at[12])
    out.start()

    @pl.when(not_last)
    def _():
        sent(kbelow.at[mine], k1s.at[0])
        for i in range(parts):
            sent(below.at[prows(i)], halo_s.at[0, i])

    @pl.when(not_first)
    def _():
        sent(kabove.at[mine], k1s.at[1])
        for i in range(parts):
            sent(above.at[prows(i)], halo_s.at[1, i])

    @pl.when(tm < steps - 1)
    def _():
        for i in range(parts):
            sent(prev.at[prows(i)], prev_s.at[i])

    sent(kbelow.at[pl.ds(0, 6 * width)], k2s)
    sent(kbelow, k3s)
    for p in range(2):
        sent(spec.at[p, pl.ds(0, count - 1)], fwd_s.at[p])
        sent(spec.at[p, pl.ds(0, count - 1)], bck_s.at[p])
    sent(fsc.at[pl.ds(0, count - 1)], fs_s)
    sent(rnc.at[pl.ds(0, count - 1)], rn_s)
    sent(edges.at[pl.ds(0, steps - 1)], ed_s)
    sent(got.at[pl.ds(0, layers - 1)], gz_s)
    take(upd, local.at[11])
    out.wait()


def body(forcing, iterate, forward_state, conductivity, terminal):
    rows, cols = iterate.shape[2:]
    steps, layers = lax.axis_size("tm"), lax.axis_size("space")
    count, half, quarter, part = steps * layers, cols // 2, cols // 4, rows // parts
    tx, ty = halves(table(cols)), halves(table(rows))
    ey = np.broadcast_to(eigen(rows)[:, None], (rows, quarter)).astype(np.float32)
    ex = np.broadcast_to(eigen(cols)[None, :], (8, cols)).astype(np.float32)
    consts = [tx, tx.transpose(0, 2, 1), ty, ty.transpose(0, 2, 1), ey, ex]
    consts = [jnp.asarray(np.ascontiguousarray(c)) for c in consts]
    V = pltpu.VMEM
    D = pltpu.SemaphoreType.DMA
    plane = V((rows, cols), f32)
    padded = V((rows + 16, cols), f32)
    scratch = [
        padded, padded, plane, plane, plane, plane, plane, plane, plane,
        V((2, cols, cols), bf16), V((2, cols, cols), bf16), V((2, rows, rows), bf16), V((2, rows, rows), bf16),
        V((rows, quarter), f32), V((8, cols), f32),
        V((part, cols), bf16), V((part, cols), bf16), V((rows, cols), bf16), V((rows, cols), bf16),
        plane, V((2, count, 8, quarter), f32), plane,
        V((8, 128), bf16), V((8, 128), bf16), V((rows, half), bf16), V((rows, half), bf16),
        plane, V((count, 8, half), f32), V((count, 8, half), f32),
        V((rows // 8 + 8, cols), f32), V((steps, 8, cols), f32), V((steps, 8, cols), f32),
        V((layers, 8, half), f32), V((layers, 8, half), f32), V((rows // steps, cols), f32),
        D((13,)), D((2, parts)), D((2, parts)), D((parts,)), D((parts,)), D((2,)), D((2,)), D, D, D, D,
        D((2,)), D((2,)), D((2,)), D((2,)), D, D, D, D, D, D, D, D,
    ]

    anywhere = pl.BlockSpec(memory_space=pl.ANY)
    rn, gr = pl.pallas_call(
        functools.partial(kernel, rows, cols, steps, layers),
        in_specs=[anywhere] * 11,
        out_specs=[anywhere] * 2,
        out_shape=[jax.ShapeDtypeStruct((rows, cols), f32), jax.ShapeDtypeStruct((rows // steps, cols), f32)],
        scratch_shapes=scratch,
        compiler_params=pltpu.CompilerParams(collective_id=0, has_side_effects=True, vmem_limit_bytes=58 << 20),
        name="correction",
    )(iterate[0, 0], forcing[0, 0], forward_state[0, 0], conductivity[0], terminal[0], *consts)
    return rn[None, None], gr[None]


def solution(mesh):
    field, layer = P("tm", "space", None, None), P("space", None, None)
    return jax.shard_map(
        body,
        mesh=mesh,
        in_specs=(field, field, field, layer, layer),
        out_specs=(field, P("space", "tm", None)),
        check_vma=False,
    )
```

```python
import functools
import math

import jax
import jax.numpy as jnp
import ml_dtypes
import numpy as np
from jax import lax
from jax.experimental import pallas as pl
from jax.experimental.pallas import tpu as pltpu
from jax.sharding import PartitionSpec as P

inv_dt = 4.0
wrap_alpha = 0.25
MESH = pl.DeviceIdType.MESH
stride = 37
parts = 4
FS1, FS2 = 40, 128
f32, bf16 = jnp.float32, jnp.bfloat16


def table(length):
    j = np.arange(length)[:, None]
    c = np.arange(length)[None, :]
    angle = math.pi * ((j * (2 * c + 1)) % (4 * length)) / (2 * length)
    factor = np.where(j == 0, math.sqrt(1.0 / length), math.sqrt(2.0 / length))
    return factor * np.cos(angle)


def eigen(length):
    return 2.0 - 2.0 * np.cos(math.pi * np.arange(length) / length)


def halves(tab):
    hi = tab.astype(ml_dtypes.bfloat16)
    lo = (tab - hi.astype(np.float64)).astype(ml_dtypes.bfloat16)
    return np.stack([hi, lo])


def split(x):
    hi = x.astype(bf16)
    return hi, (x - hi.astype(f32)).astype(bf16)


def dot3(ah, al, bh, bl):
    d = lambda a, b: jnp.dot(a, b, preferred_element_type=f32)
    return d(ah, bh) + d(ah, bl) + d(al, bh)


def take(ref, sem):
    pltpu.make_async_copy(ref, ref, sem).wait()


def kernel(rows, cols, steps, layers,
           it_h, fo_h, fs_h, ka_h, te_h, qx_h, qxt_h, qy_h, qyt_h, ey_h, ex_h,
           rn_h, gr_h,
           itv, kav, fov, fsv, below, above, kbelow, kabove,
           qx, qxt, qy, qyt, ey, ex,
           rh, rl, xh, xl, hat, spec, back, bh, bl, yh, yl, upd, fsc, rnc,
           face, edge, edges, tot, got, grad, dx, dxm, dy, dym, dz, acc5,
           local, halo_s, halo_r, k1s, k1r, k2s, k2r, k3s, k3r,
           fwd_s, fwd_r, bck_s, bck_r, fs_s, fs_r, rn_s, rn_r, ed_s, ed_r, gz_s, gz_r):
    tm, s = lax.axis_index("tm"), lax.axis_index("space")
    count = steps * layers
    me = tm * layers + s
    half, quarter = cols // 2, cols // 4
    part = rows // parts
    core, ypos, zhi = lax.rem(tm, 2), lax.rem(lax.div(tm, 2), 4), lax.div(tm, 8)

    def remote(src, dst, send, recv, to):
        return pltpu.make_async_remote_copy(src, dst, send, recv, device_id=to, device_id_type=MESH)

    def coords(d):
        return (lax.div(d, layers), lax.rem(d, layers))

    def sent(ref, sem):
        remote(ref, ref, sem, sem, (lax.rem(tm + 1, steps), s)).wait_send()

    body_it = itv.at[pl.ds(8, rows)]
    body_ka = kav.at[pl.ds(8, rows)]
    loads = [(it_h, body_it), (ka_h, body_ka), (fo_h, fov), (qxt_h, qxt), (qy_h, qy),
             (ey_h, ey), (ex_h, ex), (fs_h, fsv), (qx_h, qx), (qyt_h, qyt)]
    copies = [pltpu.make_async_copy(a, b, local.at[i]) for i, (a, b) in enumerate(loads)]
    for c in copies:
        c.start()

    barrier = pltpu.get_barrier_semaphore()

    def greet(i, c):
        pl.semaphore_signal(barrier, 1, device_id=coords(lax.rem(me + i, count)), device_id_type=MESH)
        return c

    lax.fori_loop(1, count, greet, 0)
    pl.semaphore_wait(barrier, count - 1)

    width = rows // 8

    def krows(y, c):
        return pl.ds(pl.multiple_of((y * 2 + c) * width, 8), width)

    mine = krows(ypos, core)
    not_last, not_first = s < layers - 1, s > 0
    k_up = remote(ka_h.at[mine], kbelow.at[mine], k1s.at[0], k1r.at[0], (tm, jnp.minimum(s + 1, layers - 1)))
    k_dn = remote(ka_h.at[mine], kabove.at[mine], k1s.at[1], k1r.at[1], (tm, jnp.maximum(s - 1, 0)))

    @pl.when(not_last)
    def _():
        k_up.start()

    @pl.when(not_first)
    def _():
        k_dn.start()

    @pl.when(s == 0)
    def _():
        pltpu.make_async_copy(ka_h.at[mine], kbelow.at[mine], k1r.at[0]).start()

    @pl.when(s == layers - 1)
    def _():
        pltpu.make_async_copy(ka_h.at[mine], kabove.at[mine], k1r.at[1]).start()

    def prows(i):
        return pl.ds(pl.multiple_of(i * part, 8), part)

    def halo_start(i, c):
        r = prows(i)

        @pl.when(not_last)
        def _():
            remote(it_h.at[r], below.at[r], halo_s.at[0, i], halo_r.at[0, i], (tm, jnp.minimum(s + 1, layers - 1))).start()

        @pl.when(not_first)
        def _():
            remote(it_h.at[r], above.at[r], halo_s.at[1, i], halo_r.at[1, i], (tm, jnp.maximum(s - 1, 0))).start()

        @pl.when(s == 0)
        def _():
            pltpu.make_async_copy(it_h.at[r], below.at[r], halo_r.at[0, i]).start()

        @pl.when(s == layers - 1)
        def _():
            pltpu.make_async_copy(it_h.at[r], above.at[r], halo_r.at[1, i]).start()

        return c

    lax.fori_loop(0, parts, halo_start, 0)

    for i in range(3):
        copies[i].wait()
    last = jnp.where(tm == steps - 1, 1.0, 0.0).astype(f32)
    unit = 1.0 - last
    four = inv_dt * last

    @pl.when(tm == 0)
    def _():
        term = pltpu.make_async_copy(te_h, upd, local.at[13])
        term.start()
        term.wait()

        def opening(b, c):
            r = pl.ds(pl.multiple_of(b * 8, 8), 8)
            fov[r, :] = fov[r, :] + inv_dt * upd[r, :]
            return c

        lax.fori_loop(0, rows // 8, opening, 0)

    lane = lax.broadcasted_iota(jnp.int32, (8, cols), 1)
    sub = lax.broadcasted_iota(jnp.int32, (8, cols), 0)

    def in_plane(b, c):
        r = pl.multiple_of(b * 8, 8)
        vs, ks = itv[pl.ds(r, 24), :], kav[pl.ds(r, 24), :]
        v, vu, vd = vs[8:16], vs[9:17], vs[7:15]
        k, ku, kd = ks[8:16], ks[9:17], ks[7:15]
        fx = (0.5 * (pltpu.roll(k, cols - 1, 1) + k) - unit) * (pltpu.roll(v, cols - 1, 1) - v)
        fx = jnp.where(lane == cols - 1, 0.0, fx)
        fu = jnp.where(sub + r == rows - 1, 0.0, (0.5 * (ku + k) - unit) * (vu - v))
        fd = jnp.where(sub + r == 0, 0.0, (0.5 * (k + kd) - unit) * (v - vd))
        applied = (pltpu.roll(fx, 1, 1) - fx) + (fd - fu)
        fov[pl.ds(r, 8), :] = fov[pl.ds(r, 8), :] - (four * v + applied)
        return c

    blocks = rows // 8
    lax.fori_loop(0, blocks // 4, in_plane, 0)
    take(kbelow.at[mine], k1r.at[0])
    take(kabove.at[mine], k1r.at[1])

    def along_y(i, c):
        to = (zhi * 8 + lax.rem(ypos + i, 4) * 2 + core, s)
        remote(kbelow.at[mine], kbelow.at[mine], k2s, k2r, to).start()
        remote(kabove.at[mine], kabove.at[mine], k2s, k2r, to).start()
        return c

    lax.fori_loop(1, 4, along_y, 0)
    lax.fori_loop(blocks // 4, blocks, in_plane, 0)
    take(kbelow.at[pl.ds(0, 6 * width)], k2r)

    def across(i, c):
        r = krows(i, core)
        to = (zhi * 8 + ypos * 2 + 1 - core, s)
        remote(kbelow.at[r], kbelow.at[r], k3s, k3r, to).start()
        remote(kabove.at[r], kabove.at[r], k3s, k3r, to).start()
        return c

    lax.fori_loop(0, 4, across, 0)
    take(kbelow, k3r)
    copies[3].wait()

    def fs_send(i, c):
        d = lax.rem(me + i * stride, count)
        src = fs_h.at[pl.ds(pl.multiple_of(lax.div(d, 2) * 8, 8), 8), pl.ds(pl.multiple_of(lax.rem(d, 2) * half, half), half)]
        remote(src, fsc.at[me], fs_s, fs_r, coords(d)).start()
        return c

    def arrive(i, c):
        r = prows(i)
        take(below.at[r], halo_r.at[0, i])
        take(above.at[r], halo_r.at[1, i])

        def resid(b, c):
            q = pl.multiple_of(i * part + b * 16, 16)
            at = lambda ref, off=0: ref[pl.ds(q + off, 16), :]
            v, k = at(itv, 8), at(kav, 8)
            x = at(fov) - (0.5 * (k + at(kbelow)) - unit) * (v - at(below))
            x = x - (0.5 * (k + at(kabove)) - unit) * (v - at(above))
            hi, lo = split(x)
            o = pl.multiple_of(b * 16, 16)
            rh[pl.ds(o, 16), :] = hi
            rl[pl.ds(o, 16), :] = lo
            return c

        lax.fori_loop(0, part // 16, resid, 0)
        for n in range(4):
            cs = slice(n * quarter, (n + 1) * quarter)
            acc = dot3(rh[...], rl[...], qxt[0, :, cs], qxt[1, :, cs])
            hi, lo = split(acc)
            xh[pl.ds(pl.multiple_of(i * part, 16), part), cs] = hi
            xl[pl.ds(pl.multiple_of(i * part, 16), part), cs] = lo
        return c

    lax.fori_loop(1, FS1, fs_send, 0)
    lax.fori_loop(0, parts, arrive, 0)
    copies[4].wait()

    my_rows = pl.ds(pl.multiple_of(lax.div(me, 2) * 8, 8), 8)

    def piece(d, p):
        return (pl.ds(pl.multiple_of(lax.div(d, 2) * 8, 8), 8),
                pl.ds(pl.multiple_of(p * half + lax.rem(d, 2) * quarter, quarter), quarter))

    for p in range(2):
        for n in range(2):
            cs = slice(p * half + n * quarter, p * half + (n + 1) * quarter)
            hat[:, cs] = dot3(qy[0], qy[1], xh[:, cs], xl[:, cs])

        def fwd(i, c, p=p):
            d = lax.rem(me + i * stride, count)
            remote(hat.at[piece(d, p)], spec.at[p, me], fwd_s.at[p], fwd_r.at[p], coords(d)).start()
            return c

        lax.fori_loop(1, count, fwd, 0)
        spec[p, me] = hat[piece(me, p)]

    lax.fori_loop(FS1, FS2, fs_send, 0)
    own_fs = pltpu.make_async_copy(fs_h.at[my_rows, pl.ds(pl.multiple_of(lax.rem(me, 2) * half, half), half)], fsc.at[me], local.at[10])
    own_fs.start()

    copies[5].wait()
    copies[6].wait()
    tab = table(layers)
    lam = eigen(layers)
    lz = layers // 2
    for p in range(2):
        take(spec.at[p, pl.ds(0, count - 1)], fwd_r.at[p])
        mu = ey[my_rows, :] + ex[:, pl.ds(pl.multiple_of(p * half + lax.rem(me, 2) * quarter, quarter), quarter)]
        w = [1.0 / (mu + (inv_dt + float(lam[j]))) for j in range(layers)]
        q = [inv_dt * w[j] for j in range(layers)]

        def forward(m, state, p=p, w=w, q=q):
            v = [spec[p, m * layers + z] for z in range(layers)]
            even = [v[z] + v[layers - 1 - z] for z in range(lz)]
            odd = [v[z] - v[layers - 1 - z] for z in range(lz)]
            new = []
            for j in range(layers):
                src = odd if j % 2 else even
                acc = src[0] * float(tab[j, 0])
                for z in range(1, lz):
                    acc = acc + src[z] * float(tab[j, z])
                u = q[j] * state[j] + w[j] * acc
                spec[p, m * layers + j] = u
                new.append(u)
            return tuple(new)

        state = lax.fori_loop(0, steps, forward, tuple(jnp.zeros((8, quarter), f32) for _ in range(layers)))
        carry = []
        for j in range(layers):
            t = q[j]
            for _ in range(int(math.log2(steps))):
                t = t * t
            carry.append(wrap_alpha * state[j] / (1.0 - wrap_alpha * t))

        def backward(m, carry, p=p, q=q):
            carry = tuple(q[j] * carry[j] for j in range(layers))
            u = [spec[p, m * layers + j] + carry[j] for j in range(layers)]
            for z in range(lz):
                e = u[0] * float(tab[0, z])
                o = u[1] * float(tab[1, z])
                for j in range(2, layers, 2):
                    e = e + u[j] * float(tab[j, z])
                    o = o + u[j + 1] * float(tab[j + 1, z])
                spec[p, m * layers + z] = e + o
                spec[p, m * layers + layers - 1 - z] = e - o
            return carry

        lax.fori_loop(0, steps, backward, tuple(carry))

        def bck(i, c, p=p):
            d = lax.rem(me + i * stride, count)
            remote(spec.at[p, d], back.at[piece(me, p)], bck_s.at[p], bck_r.at[p], coords(d)).start()
            return c

        lax.fori_loop(1, count, bck, 0)
        back[piece(me, p)] = spec[p, me]

    lax.fori_loop(FS2, count, fs_send, 0)
    copies[8].wait()
    copies[9].wait()

    def to_plane(p):
        take(spec.at[p, pl.ds(0, count - 1)], bck_r.at[p])
        for n in range(2):
            cs = slice(p * half + n * quarter, p * half + (n + 1) * quarter)
            hi, lo = split(back[:, cs])
            acc = dot3(qyt[0], qyt[1], hi, lo)
            hi, lo = split(acc)
            yh[:, n * quarter:(n + 1) * quarter] = hi
            yl[:, n * quarter:(n + 1) * quarter] = lo

    def along_x(p, r, n):
        cs = slice(n * quarter, (n + 1) * quarter)
        ks = slice(p * half, (p + 1) * half)
        return dot3(yh[r, :], yl[r, :], qx[0, ks, cs], qx[1, ks, cs])

    to_plane(0)

    def first(i, c):
        r = pl.ds(pl.multiple_of(i * part, 16), part)
        for n in range(4):
            cs = slice(n * quarter, (n + 1) * quarter)
            upd[r, cs] = last * itv[pl.ds(pl.multiple_of(i * part, 16) + 8, part), cs] + along_x(0, r, n)
        return c

    lax.fori_loop(0, parts, first, 0)
    to_plane(1)
    per = count // parts

    def second(i, c):
        g = lax.rem(i + tm, parts)
        start = pl.multiple_of(g * part, 16)
        r = pl.ds(start, part)
        for n in range(4):
            cs = slice(n * quarter, (n + 1) * quarter)
            upd[r, cs] = upd[r, cs] + along_x(1, r, n)

        def rn_send(j, c):
            d = g * per + lax.rem(me + j * 5, per)
            src = upd.at[pl.ds(pl.multiple_of(lax.div(d, 2) * 8, 8), 8), pl.ds(pl.multiple_of(lax.rem(d, 2) * half, half), half)]

            @pl.when(d != me)
            def _():
                remote(src, rnc.at[me], rn_s, rn_r.at[i], coords(d)).start()

            return c

        lax.fori_loop(0, per, rn_send, 0)
        pltpu.make_async_copy(upd.at[r], rn_h.at[r], local.at[11]).start()
        return c

    lax.fori_loop(0, parts, second, 0)
    rnc[me] = upd[my_rows, pl.ds(pl.multiple_of(lax.rem(me, 2) * half, half), half)]

    copies[7].wait()
    nb = rows // 8
    face[0:1, :] = jnp.zeros((1, cols), f32)
    face[pl.ds(nb, 8), :] = jnp.zeros((8, cols), f32)
    for f in range(1, nb):
        d_rn = upd[8 * f:8 * f + 1, :] - upd[8 * f - 1:8 * f, :]
        d_fs = fsv[8 * f:8 * f + 1, :] - fsv[8 * f - 1:8 * f, :]
        face[f:f + 1, :] = 0.5 * d_rn * d_fs
    tall = rows // steps
    eye = lax.broadcasted_iota(jnp.int32, (tall, 128), 0) == lax.broadcasted_iota(jnp.int32, (tall, 128), 1)
    row8 = lax.broadcasted_iota(jnp.int32, (8, cols), 0)

    for g in range(steps):
        r = slice(g * tall, (g + 1) * tall)
        d_rn = upd[r, half:half + 128] - pltpu.roll(upd[r, half - 128:half], 1, 1)
        d_fs = fsv[r, half:half + 128] - pltpu.roll(fsv[r, half - 128:half], 1, 1)
        px = 0.5 * d_rn * d_fs
        line = jnp.sum(jnp.where(eye, px[:, 0:1], 0.0), axis=0, keepdims=True)
        edge[g] = face[g * (tall // 8):g * (tall // 8) + 8, :]
        edge[g, 5:6, 0:128] = line

    def edge_send(i, c):
        g = lax.rem(tm + i, steps)
        remote(edge.at[g], edges.at[tm], ed_s, ed_r, (g, s)).start()
        return c

    lax.fori_loop(1, steps, edge_send, 0)
    edges[tm] = edge[tm]

    take(fsc.at[pl.ds(0, count - 1)], fs_r)
    own_fs.wait()
    lane8 = lax.broadcasted_iota(jnp.int32, (8, half), 1)
    sub8 = lax.broadcasted_iota(jnp.int32, (8, half), 0)

    def differences(j, c):
        b = fsc[j]
        x = jnp.where(lane8 == half - 1, 0.0, pltpu.roll(b, half - 1, 1) - b)
        dx[j] = x
        dxm[j] = pltpu.roll(x, 1, 1)
        y = jnp.where(sub8 == 7, 0.0, pltpu.roll(b, 7, 0) - b)
        dy[j] = y
        dym[j] = pltpu.roll(y, 1, 0)
        dz[j] = jnp.where(lax.rem(j, layers) == layers - 1, 0.0, fsc[jnp.minimum(j + 1, count - 1)] - b)
        return c

    lax.fori_loop(0, count, differences, 0, unroll=2)
    zone = lax.div(tm, steps // parts)
    acc5[...] = jnp.zeros_like(acc5)

    def group(i, c):
        low = lax.rem(zone - i + parts, parts)

        @pl.when(low == lax.rem(tm, parts))
        def _():
            take(rnc.at[pl.ds(0, per - 1)], rn_r.at[i])

        @pl.when(low != lax.rem(tm, parts))
        def _():
            take(rnc.at[pl.ds(0, per)], rn_r.at[i])

        def layer(z, c):
            sums = [acc5[z, f] for f in range(5)]
            for k in range(steps // parts):
                j = (low + parts * k) * layers + z
                a = rnc[j]
                up = rnc[jnp.where(z < layers - 1, j + 1, j)]
                terms = (a * dx[j], a * dxm[j], a * dy[j], a * dym[j], (up - a) * dz[j])
                sums = [p + q for p, q in zip(sums, terms)]
            for f in range(5):
                acc5[z, f] = sums[f]
            return c

        lax.fori_loop(0, layers, layer, 0)
        return c

    lax.fori_loop(0, parts, group, 0)
    fz = jnp.zeros((8, half), f32)
    for z in range(layers):
        sx, sxm, sy, sym, nz = [acc5[z, f] for f in range(5)]
        fx = (sxm - sx) + pltpu.roll(sxm, half - 1, 1) - pltpu.roll(sx, 1, 1)
        fy = (sym - sy) + pltpu.roll(sym, 7, 0) - pltpu.roll(sy, 1, 0)
        tot[z] = 0.5 * (fx + fy + fz + nz)
        fz = nz

    def tot_send(i, c):
        z = lax.rem(s + i, layers)
        remote(tot.at[z], got.at[s], gz_s, gz_r, (tm, z)).start()
        return c

    lax.fori_loop(1, layers, tot_send, 0)
    got[s] = tot[s]
    take(edges.at[pl.ds(0, steps - 1)], ed_r)
    total = edges[0]
    for t in range(1, steps):
        total = total + edges[t]
    face[0:8, :] = total
    column = jnp.sum(jnp.where(eye, face[5:6, 0:128], 0.0), axis=1, keepdims=True)
    take(got.at[pl.ds(0, layers - 1)], gz_r)
    for r in range(tall // 8):
        for h in range(2):
            cs = slice(h * half, (h + 1) * half)
            val = got[2 * r + h]
            val = val + jnp.where(sub8 == 0, face[r:r + 1, cs], 0.0)
            val = val + jnp.where(sub8 == 7, face[r + 1:r + 2, cs], 0.0)
            val = val + jnp.where(lane8 == (half - 1 if h == 0 else 0), column[8 * r:8 * r + 8], 0.0)
            grad[8 * r:8 * r + 8, cs] = val * (-1.0 / steps)
    out = pltpu.make_async_copy(grad, gr_h, local.at[12])
    out.start()

    @pl.when(not_last)
    def _():
        sent(kbelow.at[mine], k1s.at[0])
        for i in range(parts):
            sent(below.at[prows(i)], halo_s.at[0, i])

    @pl.when(not_first)
    def _():
        sent(kabove.at[mine], k1s.at[1])
        for i in range(parts):
            sent(above.at[prows(i)], halo_s.at[1, i])

    sent(kbelow.at[pl.ds(0, 6 * width)], k2s)
    sent(kbelow, k3s)
    for p in range(2):
        sent(spec.at[p, pl.ds(0, count - 1)], fwd_s.at[p])
        sent(spec.at[p, pl.ds(0, count - 1)], bck_s.at[p])
    sent(fsc.at[pl.ds(0, count - 1)], fs_s)
    sent(rnc.at[pl.ds(0, count - 1)], rn_s)
    sent(edges.at[pl.ds(0, steps - 1)], ed_s)
    sent(got.at[pl.ds(0, layers - 1)], gz_s)
    take(upd, local.at[11])
    out.wait()


def body(forcing, iterate, forward_state, conductivity, terminal):
    rows, cols = iterate.shape[2:]
    steps, layers = lax.axis_size("tm"), lax.axis_size("space")
    count, half, quarter, part = steps * layers, cols // 2, cols // 4, rows // parts
    tx, ty = halves(table(cols)), halves(table(rows))
    ey = np.broadcast_to(eigen(rows)[:, None], (rows, quarter)).astype(np.float32)
    ex = np.broadcast_to(eigen(cols)[None, :], (8, cols)).astype(np.float32)
    consts = [tx, tx.transpose(0, 2, 1), ty, ty.transpose(0, 2, 1), ey, ex]
    consts = [jnp.asarray(np.ascontiguousarray(c)) for c in consts]
    V = pltpu.VMEM
    D = pltpu.SemaphoreType.DMA
    plane = V((rows, cols), f32)
    padded = V((rows + 16, cols), f32)
    scratch = [
        padded, padded, plane, plane, plane, plane, plane, plane,
        V((2, cols, cols), bf16), V((2, cols, cols), bf16), V((2, rows, rows), bf16), V((2, rows, rows), bf16),
        V((rows, quarter), f32), V((8, cols), f32),
        V((part, cols), bf16), V((part, cols), bf16), V((rows, cols), bf16), V((rows, cols), bf16),
        plane, V((2, count, 8, quarter), f32), plane,
        V((8, 128), bf16), V((8, 128), bf16), V((rows, half), bf16), V((rows, half), bf16),
        plane, V((count, 8, half), f32), V((count, 8, half), f32),
        V((rows // 8 + 8, cols), f32), V((steps, 8, cols), f32), V((steps, 8, cols), f32),
        V((layers, 8, half), f32), V((layers, 8, half), f32), V((rows // steps, cols), f32),
        *[V((count, 8, half), f32)] * 5, V((layers, 5, 8, half), f32),
        D((14,)), D((2, parts)), D((2, parts)), D((2,)), D((2,)), D, D, D, D,
        D((2,)), D((2,)), D((2,)), D((2,)), D, D, D, D((parts,)), D, D, D, D,
    ]

    anywhere = pl.BlockSpec(memory_space=pl.ANY)
    rn, gr = pl.pallas_call(
        functools.partial(kernel, rows, cols, steps, layers),
        in_specs=[anywhere] * 11,
        out_specs=[anywhere] * 2,
        out_shape=[jax.ShapeDtypeStruct((rows, cols), f32), jax.ShapeDtypeStruct((rows // steps, cols), f32)],
        scratch_shapes=scratch,
        compiler_params=pltpu.CompilerParams(collective_id=0, has_side_effects=True, vmem_limit_bytes=60 << 20),
        name="correction",
    )(iterate[0, 0], forcing[0, 0], forward_state[0, 0], conductivity[0], terminal[0], *consts)
    return rn[None, None], gr[None]


def solution(mesh):
    field, layer = P("tm", "space", None, None), P("space", None, None)
    return jax.shard_map(
        body,
        mesh=mesh,
        in_specs=(field, field, field, layer, layer),
        out_specs=(field, P("space", "tm", None)),
        check_vma=False,
    )
```

```python
import functools
import math

import jax
import jax.numpy as jnp
import ml_dtypes
import numpy as np
from jax import lax
from jax.experimental import pallas as pl
from jax.experimental.pallas import tpu as pltpu
from jax.sharding import PartitionSpec as P

inv_dt = 4.0
wrap_alpha = 0.25
MESH = pl.DeviceIdType.MESH
stride = 37
parts = 4
FS1, FS2 = 32,96
f32, bf16 = jnp.float32, jnp.bfloat16


def table(length):
    j = np.arange(length)[:, None]
    c = np.arange(length)[None, :]
    angle = math.pi * ((j * (2 * c + 1)) % (4 * length)) / (2 * length)
    factor = np.where(j == 0, math.sqrt(1.0 / length), math.sqrt(2.0 / length))
    return factor * np.cos(angle)


def eigen(length):
    return 2.0 - 2.0 * np.cos(math.pi * np.arange(length) / length)


def halves(tab):
    hi = tab.astype(ml_dtypes.bfloat16)
    lo = (tab - hi.astype(np.float64)).astype(ml_dtypes.bfloat16)
    return np.stack([hi, lo])


def split(x):
    hi = x.astype(bf16)
    return hi, (x - hi.astype(f32)).astype(bf16)


def dot3(ah, al, bh, bl):
    d = lambda a, b: jnp.dot(a, b, preferred_element_type=f32)
    return d(ah, bh) + d(ah, bl) + d(al, bh)


def take(ref, sem):
    pltpu.make_async_copy(ref, ref, sem).wait()


def kernel(rows, cols, steps, layers,
           it_h, fo_h, fs_h, ka_h, te_h, qx_h, qxt_h, qy_h, qyt_h, ey_h, ex_h,
           rn_h, gr_h,
           itv, kav, fov, fsv, below, above, kbelow, kabove,
           qx, qxt, qy, qyt, ey, ex,
           rh, rl, xh, xl, hat, spec, back, bh, bl, yh, yl, upd, fsc, rnc,
           face, edge, edges, tot, got, grad, dx, dxm, dy, dym, dz, acc5,
           local, halo_s, halo_r, k1s, k1r, k2s, k2r, k3s, k3r,
           fwd_s, fwd_r, bck_s, bck_r, fs_s, fs_r, rn_s, rn_r, ed_s, ed_r, gz_s, gz_r):
    tm, s = lax.axis_index("tm"), lax.axis_index("space")
    count = steps * layers
    me = tm * layers + s
    half, quarter = cols // 2, cols // 4
    part = rows // parts
    core, ypos, zhi = lax.rem(tm, 2), lax.rem(lax.div(tm, 2), 4), lax.div(tm, 8)

    def remote(src, dst, send, recv, to):
        return pltpu.make_async_remote_copy(src, dst, send, recv, device_id=to, device_id_type=MESH)

    def coords(d):
        return (lax.div(d, layers), lax.rem(d, layers))

    def sent(ref, sem):
        remote(ref, ref, sem, sem, (lax.rem(tm + 1, steps), s)).wait_send()

    body_it = itv.at[pl.ds(8, rows)]
    body_ka = kav.at[pl.ds(8, rows)]
    loads = [(it_h, body_it), (ka_h, body_ka), (fo_h, fov), (qxt_h, qxt), (qy_h, qy),
             (ey_h, ey), (ex_h, ex), (fs_h, fsv), (qx_h, qx), (qyt_h, qyt)]
    copies = [pltpu.make_async_copy(a, b, local.at[i]) for i, (a, b) in enumerate(loads)]
    for c in copies:
        c.start()

    barrier = pltpu.get_barrier_semaphore()

    others = [lax.rem(s + b, layers) for b in range(layers)]
    for b in range(1, layers):
        pl.semaphore_signal(barrier, 1, device_id=(tm, others[b]), device_id_type=MESH)

    def greet(a, c):
        to = lax.rem(tm + a, steps)
        for b in range(layers):
            pl.semaphore_signal(barrier, 1, device_id=(to, others[b]), device_id_type=MESH)
        return c

    lax.fori_loop(1, steps, greet, 0)
    pl.semaphore_wait(barrier, count - 1)

    width = rows // 8

    def krows(y, c):
        return pl.ds(pl.multiple_of((y * 2 + c) * width, 8), width)

    mine = krows(ypos, core)
    not_last, not_first = s < layers - 1, s > 0
    k_up = remote(ka_h.at[mine], kbelow.at[mine], k1s.at[0], k1r.at[0], (tm, jnp.minimum(s + 1, layers - 1)))
    k_dn = remote(ka_h.at[mine], kabove.at[mine], k1s.at[1], k1r.at[1], (tm, jnp.maximum(s - 1, 0)))

    @pl.when(not_last)
    def _():
        k_up.start()

    @pl.when(not_first)
    def _():
        k_dn.start()

    @pl.when(s == 0)
    def _():
        pltpu.make_async_copy(ka_h.at[mine], kbelow.at[mine], k1r.at[0]).start()

    @pl.when(s == layers - 1)
    def _():
        pltpu.make_async_copy(ka_h.at[mine], kabove.at[mine], k1r.at[1]).start()

    def prows(i):
        return pl.ds(pl.multiple_of(i * part, 8), part)

    def halo_start(i, c):
        r = prows(i)

        @pl.when(not_last)
        def _():
            remote(it_h.at[r], below.at[r], halo_s.at[0, i], halo_r.at[0, i], (tm, jnp.minimum(s + 1, layers - 1))).start()

        @pl.when(not_first)
        def _():
            remote(it_h.at[r], above.at[r], halo_s.at[1, i], halo_r.at[1, i], (tm, jnp.maximum(s - 1, 0))).start()

        @pl.when(s == 0)
        def _():
            pltpu.make_async_copy(it_h.at[r], below.at[r], halo_r.at[0, i]).start()

        @pl.when(s == layers - 1)
        def _():
            pltpu.make_async_copy(it_h.at[r], above.at[r], halo_r.at[1, i]).start()

        return c

    lax.fori_loop(0, parts, halo_start, 0)

    for i in range(3):
        copies[i].wait()
    last = jnp.where(tm == steps - 1, 1.0, 0.0).astype(f32)
    unit = 1.0 - last
    four = inv_dt * last

    @pl.when(tm == 0)
    def _():
        term = pltpu.make_async_copy(te_h, upd, local.at[13])
        term.start()
        term.wait()

        def opening(b, c):
            r = pl.ds(pl.multiple_of(b * 8, 8), 8)
            fov[r, :] = fov[r, :] + inv_dt * upd[r, :]
            return c

        lax.fori_loop(0, rows // 8, opening, 0)

    lane = lax.broadcasted_iota(jnp.int32, (8, cols), 1)
    sub = lax.broadcasted_iota(jnp.int32, (8, cols), 0)

    def in_plane(b, c):
        r = pl.multiple_of(b * 8, 8)
        vs, ks = itv[pl.ds(r, 24), :], kav[pl.ds(r, 24), :]
        v, vu, vd = vs[8:16], vs[9:17], vs[7:15]
        k, ku, kd = ks[8:16], ks[9:17], ks[7:15]
        fx = (0.5 * (pltpu.roll(k, cols - 1, 1) + k) - unit) * (pltpu.roll(v, cols - 1, 1) - v)
        fx = jnp.where(lane == cols - 1, 0.0, fx)
        fu = jnp.where(sub + r == rows - 1, 0.0, (0.5 * (ku + k) - unit) * (vu - v))
        fd = jnp.where(sub + r == 0, 0.0, (0.5 * (k + kd) - unit) * (v - vd))
        applied = (pltpu.roll(fx, 1, 1) - fx) + (fd - fu)
        fov[pl.ds(r, 8), :] = fov[pl.ds(r, 8), :] - (four * v + applied)
        return c

    blocks = rows // 8
    lax.fori_loop(0, blocks // 4, in_plane, 0)
    take(kbelow.at[mine], k1r.at[0])
    take(kabove.at[mine], k1r.at[1])

    def along_y(i, c):
        to = (zhi * 8 + lax.rem(ypos + i, 4) * 2 + core, s)
        remote(kbelow.at[mine], kbelow.at[mine], k2s, k2r, to).start()
        remote(kabove.at[mine], kabove.at[mine], k2s, k2r, to).start()
        return c

    lax.fori_loop(1, 4, along_y, 0)
    lax.fori_loop(blocks // 4, blocks, in_plane, 0)
    take(kbelow.at[pl.ds(0, 6 * width)], k2r)

    def across(i, c):
        r = krows(i, core)
        to = (zhi * 8 + ypos * 2 + 1 - core, s)
        remote(kbelow.at[r], kbelow.at[r], k3s, k3r, to).start()
        remote(kabove.at[r], kabove.at[r], k3s, k3r, to).start()
        return c

    lax.fori_loop(0, 4, across, 0)
    take(kbelow, k3r)
    copies[3].wait()

    def fs_send(i, c):
        d = lax.rem(me + i * stride, count)
        src = fs_h.at[pl.ds(pl.multiple_of(lax.div(d, 2) * 8, 8), 8), pl.ds(pl.multiple_of(lax.rem(d, 2) * half, half), half)]
        remote(src, fsc.at[me], fs_s, fs_r, coords(d)).start()
        return c

    def arrive(i, c):
        r = prows(i)
        take(below.at[r], halo_r.at[0, i])
        take(above.at[r], halo_r.at[1, i])

        def resid(b, c):
            q = pl.multiple_of(i * part + b * 16, 16)
            at = lambda ref, off=0: ref[pl.ds(q + off, 16), :]
            v, k = at(itv, 8), at(kav, 8)
            x = at(fov) - (0.5 * (k + at(kbelow)) - unit) * (v - at(below))
            x = x - (0.5 * (k + at(kabove)) - unit) * (v - at(above))
            hi, lo = split(x)
            o = pl.multiple_of(b * 16, 16)
            rh[pl.ds(o, 16), :] = hi
            rl[pl.ds(o, 16), :] = lo
            return c

        lax.fori_loop(0, part // 16, resid, 0)
        for n in range(4):
            cs = slice(n * quarter, (n + 1) * quarter)
            acc = dot3(rh[...], rl[...], qxt[0, :, cs], qxt[1, :, cs])
            hi, lo = split(acc)
            xh[pl.ds(pl.multiple_of(i * part, 16), part), cs] = hi
            xl[pl.ds(pl.multiple_of(i * part, 16), part), cs] = lo
        return c

    lax.fori_loop(1, FS1, fs_send, 0)
    lax.fori_loop(0, parts, arrive, 0)
    copies[4].wait()

    my_rows = pl.ds(pl.multiple_of(lax.div(me, 2) * 8, 8), 8)

    def piece(d, p):
        return (pl.ds(pl.multiple_of(lax.div(d, 2) * 8, 8), 8),
                pl.ds(pl.multiple_of(p * half + lax.rem(d, 2) * quarter, quarter), quarter))

    for p in range(2):
        for n in range(2):
            cs = slice(p * half + n * quarter, p * half + (n + 1) * quarter)
            hat[:, cs] = dot3(qy[0], qy[1], xh[:, cs], xl[:, cs])

        def fwd(i, c, p=p):
            d = lax.rem(me + i * stride, count)
            remote(hat.at[piece(d, p)], spec.at[p, me], fwd_s.at[p], fwd_r.at[p], coords(d)).start()
            return c

        lax.fori_loop(1, count, fwd, 0)
        spec[p, me] = hat[piece(me, p)]

    lax.fori_loop(FS1, FS2, fs_send, 0)
    own_fs = pltpu.make_async_copy(fs_h.at[my_rows, pl.ds(pl.multiple_of(lax.rem(me, 2) * half, half), half)], fsc.at[me], local.at[10])
    own_fs.start()

    copies[5].wait()
    copies[6].wait()
    tab = table(layers)
    lam = eigen(layers)
    lz = layers // 2
    for p in range(2):
        take(spec.at[p, pl.ds(0, count - 1)], fwd_r.at[p])
        mu = ey[my_rows, :] + ex[:, pl.ds(pl.multiple_of(p * half + lax.rem(me, 2) * quarter, quarter), quarter)]
        w = [1.0 / (mu + (inv_dt + float(lam[j]))) for j in range(layers)]
        q = [inv_dt * w[j] for j in range(layers)]

        def forward(m, state, p=p, w=w, q=q):
            v = [spec[p, m * layers + z] for z in range(layers)]
            even = [v[z] + v[layers - 1 - z] for z in range(lz)]
            odd = [v[z] - v[layers - 1 - z] for z in range(lz)]
            new = []
            for j in range(layers):
                src = odd if j % 2 else even
                acc = src[0] * float(tab[j, 0])
                for z in range(1, lz):
                    acc = acc + src[z] * float(tab[j, z])
                u = q[j] * state[j] + w[j] * acc
                spec[p, m * layers + j] = u
                new.append(u)
            return tuple(new)

        state = lax.fori_loop(0, steps, forward, tuple(jnp.zeros((8, quarter), f32) for _ in range(layers)))
        carry = []
        for j in range(layers):
            t = q[j]
            for _ in range(int(math.log2(steps))):
                t = t * t
            carry.append(wrap_alpha * state[j] / (1.0 - wrap_alpha * t))

        def backward(m, carry, p=p, q=q):
            carry = tuple(q[j] * carry[j] for j in range(layers))
            u = [spec[p, m * layers + j] + carry[j] for j in range(layers)]
            for z in range(lz):
                e = u[0] * float(tab[0, z])
                o = u[1] * float(tab[1, z])
                for j in range(2, layers, 2):
                    e = e + u[j] * float(tab[j, z])
                    o = o + u[j + 1] * float(tab[j + 1, z])
                spec[p, m * layers + z] = e + o
                spec[p, m * layers + layers - 1 - z] = e - o
            return carry

        lax.fori_loop(0, steps, backward, tuple(carry))

        def bck(i, c, p=p):
            d = lax.rem(me + i * stride, count)
            remote(spec.at[p, d], back.at[piece(me, p)], bck_s.at[p], bck_r.at[p], coords(d)).start()
            return c

        lax.fori_loop(1, count, bck, 0)
        back[piece(me, p)] = spec[p, me]

    lax.fori_loop(FS2, count, fs_send, 0)
    copies[8].wait()
    copies[9].wait()

    def to_plane(p):
        take(spec.at[p, pl.ds(0, count - 1)], bck_r.at[p])
        for n in range(2):
            cs = slice(p * half + n * quarter, p * half + (n + 1) * quarter)
            hi, lo = split(back[:, cs])
            acc = dot3(qyt[0], qyt[1], hi, lo)
            hi, lo = split(acc)
            yh[:, n * quarter:(n + 1) * quarter] = hi
            yl[:, n * quarter:(n + 1) * quarter] = lo

    def along_x(p, r, n):
        cs = slice(n * quarter, (n + 1) * quarter)
        ks = slice(p * half, (p + 1) * half)
        return dot3(yh[r, :], yl[r, :], qx[0, ks, cs], qx[1, ks, cs])

    to_plane(0)

    def first(i, c):
        r = pl.ds(pl.multiple_of(i * part, 16), part)
        for n in range(4):
            cs = slice(n * quarter, (n + 1) * quarter)
            upd[r, cs] = last * itv[pl.ds(pl.multiple_of(i * part, 16) + 8, part), cs] + along_x(0, r, n)
        return c

    lax.fori_loop(0, parts, first, 0)
    to_plane(1)
    per = count // parts

    def second(i, c):
        g = lax.rem(i + tm, parts)
        start = pl.multiple_of(g * part, 16)
        r = pl.ds(start, part)
        for n in range(4):
            cs = slice(n * quarter, (n + 1) * quarter)
            upd[r, cs] = upd[r, cs] + along_x(1, r, n)

        def rn_send(j, c):
            d = g * per + lax.rem(me + j * 5, per)
            src = upd.at[pl.ds(pl.multiple_of(lax.div(d, 2) * 8, 8), 8), pl.ds(pl.multiple_of(lax.rem(d, 2) * half, half), half)]

            @pl.when(d != me)
            def _():
                remote(src, rnc.at[me], rn_s, rn_r.at[i], coords(d)).start()

            return c

        lax.fori_loop(0, per, rn_send, 0)
        pltpu.make_async_copy(upd.at[r], rn_h.at[r], local.at[11]).start()
        return c

    lax.fori_loop(0, parts, second, 0)
    rnc[me] = upd[my_rows, pl.ds(pl.multiple_of(lax.rem(me, 2) * half, half), half)]

    copies[7].wait()
    nb = rows // 8
    face[0:1, :] = jnp.zeros((1, cols), f32)
    face[pl.ds(nb, 8), :] = jnp.zeros((8, cols), f32)
    for f in range(1, nb):
        d_rn = upd[8 * f:8 * f + 1, :] - upd[8 * f - 1:8 * f, :]
        d_fs = fsv[8 * f:8 * f + 1, :] - fsv[8 * f - 1:8 * f, :]
        face[f:f + 1, :] = 0.5 * d_rn * d_fs
    tall = rows // steps
    eye = lax.broadcasted_iota(jnp.int32, (tall, 128), 0) == lax.broadcasted_iota(jnp.int32, (tall, 128), 1)
    row8 = lax.broadcasted_iota(jnp.int32, (8, cols), 0)

    for g in range(steps):
        r = slice(g * tall, (g + 1) * tall)
        d_rn = upd[r, half:half + 128] - pltpu.roll(upd[r, half - 128:half], 1, 1)
        d_fs = fsv[r, half:half + 128] - pltpu.roll(fsv[r, half - 128:half], 1, 1)
        px = 0.5 * d_rn * d_fs
        line = jnp.sum(jnp.where(eye, px[:, 0:1], 0.0), axis=0, keepdims=True)
        edge[g] = face[g * (tall // 8):g * (tall // 8) + 8, :]
        edge[g, 5:6, 0:128] = line

    def edge_send(i, c):
        g = lax.rem(tm + i, steps)
        remote(edge.at[g], edges.at[tm], ed_s, ed_r, (g, s)).start()
        return c

    lax.fori_loop(1, steps, edge_send, 0)
    edges[tm] = edge[tm]

    take(fsc.at[pl.ds(0, count - 1)], fs_r)
    own_fs.wait()
    lane8 = lax.broadcasted_iota(jnp.int32, (8, half), 1)
    sub8 = lax.broadcasted_iota(jnp.int32, (8, half), 0)

    def differences(j, c):
        b = fsc[j]
        x = jnp.where(lane8 == half - 1, 0.0, pltpu.roll(b, half - 1, 1) - b)
        dx[j] = x
        dxm[j] = pltpu.roll(x, 1, 1)
        y = jnp.where(sub8 == 7, 0.0, pltpu.roll(b, 7, 0) - b)
        dy[j] = y
        dym[j] = pltpu.roll(y, 1, 0)
        dz[j] = jnp.where(lax.rem(j, layers) == layers - 1, 0.0, fsc[jnp.minimum(j + 1, count - 1)] - b)
        return c

    lax.fori_loop(0, count, differences, 0, unroll=2)
    zone = lax.div(tm, steps // parts)
    acc5[...] = jnp.zeros_like(acc5)

    def group(i, c):
        low = lax.rem(zone - i + parts, parts)

        @pl.when(low == lax.rem(tm, parts))
        def _():
            take(rnc.at[pl.ds(0, per - 1)], rn_r.at[i])

        @pl.when(low != lax.rem(tm, parts))
        def _():
            take(rnc.at[pl.ds(0, per)], rn_r.at[i])

        def layer(z, c):
            sums = [acc5[z, f] for f in range(5)]
            for k in range(steps // parts):
                j = (low + parts * k) * layers + z
                a = rnc[j]
                up = rnc[jnp.where(z < layers - 1, j + 1, j)]
                terms = (a * dx[j], a * dxm[j], a * dy[j], a * dym[j], (up - a) * dz[j])
                sums = [p + q for p, q in zip(sums, terms)]
            for f in range(5):
                acc5[z, f] = sums[f]
            return c

        lax.fori_loop(0, layers, layer, 0)
        return c

    lax.fori_loop(0, parts, group, 0)
    fz = jnp.zeros((8, half), f32)
    for z in range(layers):
        sx, sxm, sy, sym, nz = [acc5[z, f] for f in range(5)]
        fx = (sxm - sx) + pltpu.roll(sxm, half - 1, 1) - pltpu.roll(sx, 1, 1)
        fy = (sym - sy) + pltpu.roll(sym, 7, 0) - pltpu.roll(sy, 1, 0)
        tot[z] = 0.5 * (fx + fy + fz + nz)
        fz = nz

    def tot_send(i, c):
        z = lax.rem(s + i, layers)
        remote(tot.at[z], got.at[s], gz_s, gz_r, (tm, z)).start()
        return c

    lax.fori_loop(1, layers, tot_send, 0)
    got[s] = tot[s]
    take(edges.at[pl.ds(0, steps - 1)], ed_r)
    total = edges[0]
    for t in range(1, steps):
        total = total + edges[t]
    face[0:8, :] = total
    column = jnp.sum(jnp.where(eye, face[5:6, 0:128], 0.0), axis=1, keepdims=True)
    take(got.at[pl.ds(0, layers - 1)], gz_r)
    for r in range(tall // 8):
        for h in range(2):
            cs = slice(h * half, (h + 1) * half)
            val = got[2 * r + h]
            val = val + jnp.where(sub8 == 0, face[r:r + 1, cs], 0.0)
            val = val + jnp.where(sub8 == 7, face[r + 1:r + 2, cs], 0.0)
            val = val + jnp.where(lane8 == (half - 1 if h == 0 else 0), column[8 * r:8 * r + 8], 0.0)
            grad[8 * r:8 * r + 8, cs] = val * (-1.0 / steps)
    out = pltpu.make_async_copy(grad, gr_h, local.at[12])
    out.start()

    @pl.when(not_last)
    def _():
        sent(kbelow.at[mine], k1s.at[0])
        for i in range(parts):
            sent(below.at[prows(i)], halo_s.at[0, i])

    @pl.when(not_first)
    def _():
        sent(kabove.at[mine], k1s.at[1])
        for i in range(parts):
            sent(above.at[prows(i)], halo_s.at[1, i])

    sent(kbelow.at[pl.ds(0, 6 * width)], k2s)
    sent(kbelow, k3s)
    for p in range(2):
        sent(spec.at[p, pl.ds(0, count - 1)], fwd_s.at[p])
        sent(spec.at[p, pl.ds(0, count - 1)], bck_s.at[p])
    sent(fsc.at[pl.ds(0, count - 1)], fs_s)
    sent(rnc.at[pl.ds(0, count - 1)], rn_s)
    sent(edges.at[pl.ds(0, steps - 1)], ed_s)
    sent(got.at[pl.ds(0, layers - 1)], gz_s)
    take(upd, local.at[11])
    out.wait()


def body(forcing, iterate, forward_state, conductivity, terminal):
    rows, cols = iterate.shape[2:]
    steps, layers = lax.axis_size("tm"), lax.axis_size("space")
    count, half, quarter, part = steps * layers, cols // 2, cols // 4, rows // parts
    tx, ty = halves(table(cols)), halves(table(rows))
    ey = np.broadcast_to(eigen(rows)[:, None], (rows, quarter)).astype(np.float32)
    ex = np.broadcast_to(eigen(cols)[None, :], (8, cols)).astype(np.float32)
    consts = [tx, tx.transpose(0, 2, 1), ty, ty.transpose(0, 2, 1), ey, ex]
    consts = [jnp.asarray(np.ascontiguousarray(c)) for c in consts]
    V = pltpu.VMEM
    D = pltpu.SemaphoreType.DMA
    plane = V((rows, cols), f32)
    padded = V((rows + 16, cols), f32)
    scratch = [
        padded, padded, plane, plane, plane, plane, plane, plane,
        V((2, cols, cols), bf16), V((2, cols, cols), bf16), V((2, rows, rows), bf16), V((2, rows, rows), bf16),
        V((rows, quarter), f32), V((8, cols), f32),
        V((part, cols), bf16), V((part, cols), bf16), V((rows, cols), bf16), V((rows, cols), bf16),
        plane, V((2, count, 8, quarter), f32), plane,
        V((8, 128), bf16), V((8, 128), bf16), V((rows, half), bf16), V((rows, half), bf16),
        plane, V((count, 8, half), f32), V((count, 8, half), f32),
        V((rows // 8 + 8, cols), f32), V((steps, 8, cols), f32), V((steps, 8, cols), f32),
        V((layers, 8, half), f32), V((layers, 8, half), f32), V((rows // steps, cols), f32),
        *[V((count, 8, half), f32)] * 5, V((layers, 5, 8, half), f32),
        D((14,)), D((2, parts)), D((2, parts)), D((2,)), D((2,)), D, D, D, D,
        D((2,)), D((2,)), D((2,)), D((2,)), D, D, D, D((parts,)), D, D, D, D,
    ]

    anywhere = pl.BlockSpec(memory_space=pl.ANY)
    rn, gr = pl.pallas_call(
        functools.partial(kernel, rows, cols, steps, layers),
        in_specs=[anywhere] * 11,
        out_specs=[anywhere] * 2,
        out_shape=[jax.ShapeDtypeStruct((rows, cols), f32), jax.ShapeDtypeStruct((rows // steps, cols), f32)],
        scratch_shapes=scratch,
        compiler_params=pltpu.CompilerParams(collective_id=0, has_side_effects=True, vmem_limit_bytes=60 << 20),
        name="correction",
    )(iterate[0, 0], forcing[0, 0], forward_state[0, 0], conductivity[0], terminal[0], *consts)
    return rn[None, None], gr[None]


def solution(mesh):
    field, layer = P("tm", "space", None, None), P("space", None, None)
    return jax.shard_map(
        body,
        mesh=mesh,
        in_specs=(field, field, field, layer, layer),
        out_specs=(field, P("space", "tm", None)),
        check_vma=False,
    )
```

```python
import functools
import math

import jax
import jax.numpy as jnp
import ml_dtypes
import numpy as np
from jax import lax
from jax.experimental import pallas as pl
from jax.experimental.pallas import tpu as pltpu
from jax.sharding import PartitionSpec as P

inv_dt = 4.0
wrap_alpha = 0.25
MESH = pl.DeviceIdType.MESH
stride = 37
parts = 4
FS1, FS2 = 32,96
f32, bf16 = jnp.float32, jnp.bfloat16


def table(length):
    j = np.arange(length)[:, None]
    c = np.arange(length)[None, :]
    angle = math.pi * ((j * (2 * c + 1)) % (4 * length)) / (2 * length)
    factor = np.where(j == 0, math.sqrt(1.0 / length), math.sqrt(2.0 / length))
    return factor * np.cos(angle)


def eigen(length):
    return 2.0 - 2.0 * np.cos(math.pi * np.arange(length) / length)


def halves(tab):
    hi = tab.astype(ml_dtypes.bfloat16)
    lo = (tab - hi.astype(np.float64)).astype(ml_dtypes.bfloat16)
    return np.stack([hi, lo])


def split(x):
    hi = x.astype(bf16)
    return hi, (x - hi.astype(f32)).astype(bf16)


def dot3(ah, al, bh, bl):
    d = lambda a, b: jnp.dot(a, b, preferred_element_type=f32)
    return d(ah, bh) + d(ah, bl) + d(al, bh)


def take(ref, sem):
    pltpu.make_async_copy(ref, ref, sem).wait()


def kernel(rows, cols, steps, layers,
           it_h, fo_h, fs_h, ka_h, te_h, tab_h, eig_h,
           rn_h, gr_h,
           itv, kav, fov, fsv, below, above, kbelow, kabove,
           qx, qxt, qy, qyt, ey, ex,
           rh, rl, xh, xl, hat, spec, back, bh, bl, yh, yl, upd, fsc, rnc,
           face, edge, edges, tot, got, grad, acc5,
           local, halo_s, halo_r, k1s, k1r, k2s, k2r, k3s, k3r,
           fwd_s, fwd_r, bck_s, bck_r, fs_s, fs_r, rn_s, rn_r, ed_s, ed_r, gz_s, gz_r):
    tm, s = lax.axis_index("tm"), lax.axis_index("space")
    count = steps * layers
    me = tm * layers + s
    half, quarter = cols // 2, cols // 4
    part = rows // parts
    core, ypos, zhi = lax.rem(tm, 2), lax.rem(lax.div(tm, 2), 4), lax.div(tm, 8)

    def remote(src, dst, send, recv, to):
        return pltpu.make_async_remote_copy(src, dst, send, recv, device_id=to, device_id_type=MESH)

    def coords(d):
        return (lax.div(d, layers), lax.rem(d, layers))

    def sent(ref, sem):
        remote(ref, ref, sem, sem, (lax.rem(tm + 1, steps), s)).wait_send()

    qx_h, qxt_h = tab_h.at[0:2], tab_h.at[2:4]
    qy_h = tab_h.at[4:6, 0:rows, 0:rows]
    qyt_h = tab_h.at[4:6, 0:rows, rows:2 * rows]
    ey_h, ex_h = eig_h.at[0:rows, 0:quarter], eig_h.at[rows:rows + 8]
    body_it = itv.at[pl.ds(8, rows)]
    body_ka = kav.at[pl.ds(8, rows)]
    loads = [(it_h, body_it), (ka_h, body_ka), (fo_h, fov), (qxt_h, qxt), (qy_h, qy),
             (ey_h, ey), (ex_h, ex), (fs_h, fsv), (qx_h, qx), (qyt_h, qyt)]
    copies = [pltpu.make_async_copy(a, b, local.at[i]) for i, (a, b) in enumerate(loads)]
    for c in copies:
        c.start()

    barrier = pltpu.get_barrier_semaphore()

    others = [lax.rem(s + b, layers) for b in range(layers)]
    for b in range(1, layers):
        pl.semaphore_signal(barrier, 1, device_id=(tm, others[b]), device_id_type=MESH)

    def greet(a, c):
        to = lax.rem(tm + a, steps)
        for b in range(layers):
            pl.semaphore_signal(barrier, 1, device_id=(to, others[b]), device_id_type=MESH)
        return c

    lax.fori_loop(1, steps, greet, 0)
    pl.semaphore_wait(barrier, count - 1)

    width = rows // 8

    def krows(y, c):
        return pl.ds(pl.multiple_of((y * 2 + c) * width, 8), width)

    mine = krows(ypos, core)
    not_last, not_first = s < layers - 1, s > 0
    k_up = remote(ka_h.at[mine], kbelow.at[mine], k1s.at[0], k1r.at[0], (tm, jnp.minimum(s + 1, layers - 1)))
    k_dn = remote(ka_h.at[mine], kabove.at[mine], k1s.at[1], k1r.at[1], (tm, jnp.maximum(s - 1, 0)))

    @pl.when(not_last)
    def _():
        k_up.start()

    @pl.when(not_first)
    def _():
        k_dn.start()

    @pl.when(s == 0)
    def _():
        pltpu.make_async_copy(ka_h.at[mine], kbelow.at[mine], k1r.at[0]).start()

    @pl.when(s == layers - 1)
    def _():
        pltpu.make_async_copy(ka_h.at[mine], kabove.at[mine], k1r.at[1]).start()

    def prows(i):
        return pl.ds(pl.multiple_of(i * part, 8), part)

    def halo_start(i, c):
        r = prows(i)

        @pl.when(not_last)
        def _():
            remote(it_h.at[r], below.at[r], halo_s.at[0, i], halo_r.at[0, i], (tm, jnp.minimum(s + 1, layers - 1))).start()

        @pl.when(not_first)
        def _():
            remote(it_h.at[r], above.at[r], halo_s.at[1, i], halo_r.at[1, i], (tm, jnp.maximum(s - 1, 0))).start()

        @pl.when(s == 0)
        def _():
            pltpu.make_async_copy(it_h.at[r], below.at[r], halo_r.at[0, i]).start()

        @pl.when(s == layers - 1)
        def _():
            pltpu.make_async_copy(it_h.at[r], above.at[r], halo_r.at[1, i]).start()

        return c

    lax.fori_loop(0, parts, halo_start, 0)

    for i in range(3):
        copies[i].wait()
    last = jnp.where(tm == steps - 1, 1.0, 0.0).astype(f32)
    unit = 1.0 - last
    four = inv_dt * last

    @pl.when(tm == 0)
    def _():
        term = pltpu.make_async_copy(te_h, upd, local.at[13])
        term.start()
        term.wait()

        def opening(b, c):
            r = pl.ds(pl.multiple_of(b * 8, 8), 8)
            fov[r, :] = fov[r, :] + inv_dt * upd[r, :]
            return c

        lax.fori_loop(0, rows // 8, opening, 0)

    lane = lax.broadcasted_iota(jnp.int32, (8, cols), 1)
    sub = lax.broadcasted_iota(jnp.int32, (8, cols), 0)

    def in_plane(b, c):
        r = pl.multiple_of(b * 8, 8)
        vs, ks = itv[pl.ds(r, 24), :], kav[pl.ds(r, 24), :]
        v, vu, vd = vs[8:16], vs[9:17], vs[7:15]
        k, ku, kd = ks[8:16], ks[9:17], ks[7:15]
        fx = (0.5 * (pltpu.roll(k, cols - 1, 1) + k) - unit) * (pltpu.roll(v, cols - 1, 1) - v)
        fx = jnp.where(lane == cols - 1, 0.0, fx)
        fu = jnp.where(sub + r == rows - 1, 0.0, (0.5 * (ku + k) - unit) * (vu - v))
        fd = jnp.where(sub + r == 0, 0.0, (0.5 * (k + kd) - unit) * (v - vd))
        applied = (pltpu.roll(fx, 1, 1) - fx) + (fd - fu)
        fov[pl.ds(r, 8), :] = fov[pl.ds(r, 8), :] - (four * v + applied)
        return c

    blocks = rows // 8
    lax.fori_loop(0, blocks // 4, in_plane, 0)
    take(kbelow.at[mine], k1r.at[0])
    take(kabove.at[mine], k1r.at[1])

    def along_y(i, c):
        to = (zhi * 8 + lax.rem(ypos + i, 4) * 2 + core, s)
        remote(kbelow.at[mine], kbelow.at[mine], k2s, k2r, to).start()
        remote(kabove.at[mine], kabove.at[mine], k2s, k2r, to).start()
        return c

    lax.fori_loop(1, 4, along_y, 0)
    lax.fori_loop(blocks // 4, blocks, in_plane, 0)
    take(kbelow.at[pl.ds(0, 6 * width)], k2r)

    def across(i, c):
        r = krows(i, core)
        to = (zhi * 8 + ypos * 2 + 1 - core, s)
        remote(kbelow.at[r], kbelow.at[r], k3s, k3r, to).start()
        remote(kabove.at[r], kabove.at[r], k3s, k3r, to).start()
        return c

    lax.fori_loop(0, 4, across, 0)
    take(kbelow, k3r)
    copies[3].wait()

    def fs_send(i, c):
        d = lax.rem(me + i * stride, count)
        src = fs_h.at[pl.ds(pl.multiple_of(lax.div(d, 2) * 8, 8), 8), pl.ds(pl.multiple_of(lax.rem(d, 2) * half, half), half)]
        remote(src, fsc.at[me], fs_s, fs_r, coords(d)).start()
        return c

    def arrive(i, c):
        r = prows(i)
        take(below.at[r], halo_r.at[0, i])
        take(above.at[r], halo_r.at[1, i])

        def resid(b, c):
            q = pl.multiple_of(i * part + b * 16, 16)
            at = lambda ref, off=0: ref[pl.ds(q + off, 16), :]
            v, k = at(itv, 8), at(kav, 8)
            x = at(fov) - (0.5 * (k + at(kbelow)) - unit) * (v - at(below))
            x = x - (0.5 * (k + at(kabove)) - unit) * (v - at(above))
            hi, lo = split(x)
            o = pl.multiple_of(b * 16, 16)
            rh[pl.ds(o, 16), :] = hi
            rl[pl.ds(o, 16), :] = lo
            return c

        lax.fori_loop(0, part // 16, resid, 0)
        for n in range(4):
            cs = slice(n * quarter, (n + 1) * quarter)
            acc = dot3(rh[...], rl[...], qxt[0, :, cs], qxt[1, :, cs])
            hi, lo = split(acc)
            xh[pl.ds(pl.multiple_of(i * part, 16), part), cs] = hi
            xl[pl.ds(pl.multiple_of(i * part, 16), part), cs] = lo
        return c

    lax.fori_loop(1, FS1, fs_send, 0)
    lax.fori_loop(0, parts, arrive, 0)
    copies[4].wait()

    my_rows = pl.ds(pl.multiple_of(lax.div(me, 2) * 8, 8), 8)

    def piece(d, p):
        return (pl.ds(pl.multiple_of(lax.div(d, 2) * 8, 8), 8),
                pl.ds(pl.multiple_of(p * half + lax.rem(d, 2) * quarter, quarter), quarter))

    for p in range(2):
        for n in range(2):
            cs = slice(p * half + n * quarter, p * half + (n + 1) * quarter)
            hat[:, cs] = dot3(qy[0], qy[1], xh[:, cs], xl[:, cs])

        def fwd(i, c, p=p):
            d = lax.rem(me + i * stride, count)
            remote(hat.at[piece(d, p)], spec.at[p, me], fwd_s.at[p], fwd_r.at[p], coords(d)).start()
            return c

        lax.fori_loop(1, count, fwd, 0)
        spec[p, me] = hat[piece(me, p)]

    lax.fori_loop(FS1, FS2, fs_send, 0)
    own_fs = pltpu.make_async_copy(fs_h.at[my_rows, pl.ds(pl.multiple_of(lax.rem(me, 2) * half, half), half)], fsc.at[me], local.at[10])
    own_fs.start()

    copies[5].wait()
    copies[6].wait()
    tab = table(layers)
    lam = eigen(layers)
    lz = layers // 2
    for p in range(2):
        take(spec.at[p, pl.ds(0, count - 1)], fwd_r.at[p])
        mu = ey[my_rows, :] + ex[:, pl.ds(pl.multiple_of(p * half + lax.rem(me, 2) * quarter, quarter), quarter)]
        w = [1.0 / (mu + (inv_dt + float(lam[j]))) for j in range(layers)]
        q = [inv_dt * w[j] for j in range(layers)]

        def forward(m, state, p=p, w=w, q=q):
            v = [spec[p, m * layers + z] for z in range(layers)]
            even = [v[z] + v[layers - 1 - z] for z in range(lz)]
            odd = [v[z] - v[layers - 1 - z] for z in range(lz)]
            new = []
            for j in range(layers):
                src = odd if j % 2 else even
                acc = src[0] * float(tab[j, 0])
                for z in range(1, lz):
                    acc = acc + src[z] * float(tab[j, z])
                u = q[j] * state[j] + w[j] * acc
                spec[p, m * layers + j] = u
                new.append(u)
            return tuple(new)

        state = lax.fori_loop(0, steps, forward, tuple(jnp.zeros((8, quarter), f32) for _ in range(layers)))
        carry = []
        for j in range(layers):
            t = q[j]
            for _ in range(int(math.log2(steps))):
                t = t * t
            carry.append(wrap_alpha * state[j] / (1.0 - wrap_alpha * t))

        def backward(m, carry, p=p, q=q):
            carry = tuple(q[j] * carry[j] for j in range(layers))
            u = [spec[p, m * layers + j] + carry[j] for j in range(layers)]
            for z in range(lz):
                e = u[0] * float(tab[0, z])
                o = u[1] * float(tab[1, z])
                for j in range(2, layers, 2):
                    e = e + u[j] * float(tab[j, z])
                    o = o + u[j + 1] * float(tab[j + 1, z])
                spec[p, m * layers + z] = e + o
                spec[p, m * layers + layers - 1 - z] = e - o
            return carry

        lax.fori_loop(0, steps, backward, tuple(carry))

        def bck(i, c, p=p):
            d = lax.rem(me + i * stride, count)
            remote(spec.at[p, d], back.at[piece(me, p)], bck_s.at[p], bck_r.at[p], coords(d)).start()
            return c

        lax.fori_loop(1, count, bck, 0)
        back[piece(me, p)] = spec[p, me]

    lax.fori_loop(FS2, count, fs_send, 0)
    copies[8].wait()
    copies[9].wait()

    def to_plane(p):
        take(spec.at[p, pl.ds(0, count - 1)], bck_r.at[p])
        for n in range(2):
            cs = slice(p * half + n * quarter, p * half + (n + 1) * quarter)
            hi, lo = split(back[:, cs])
            acc = dot3(qyt[0], qyt[1], hi, lo)
            hi, lo = split(acc)
            yh[:, n * quarter:(n + 1) * quarter] = hi
            yl[:, n * quarter:(n + 1) * quarter] = lo

    def along_x(p, r, n):
        cs = slice(n * quarter, (n + 1) * quarter)
        ks = slice(p * half, (p + 1) * half)
        return dot3(yh[r, :], yl[r, :], qx[0, ks, cs], qx[1, ks, cs])

    to_plane(0)

    def first(i, c):
        r = pl.ds(pl.multiple_of(i * part, 16), part)
        for n in range(4):
            cs = slice(n * quarter, (n + 1) * quarter)
            upd[r, cs] = last * itv[pl.ds(pl.multiple_of(i * part, 16) + 8, part), cs] + along_x(0, r, n)
        return c

    lax.fori_loop(0, parts, first, 0)
    to_plane(1)
    per = count // parts

    def second(i, c):
        g = lax.rem(i + tm, parts)
        start = pl.multiple_of(g * part, 16)
        r = pl.ds(start, part)
        for n in range(4):
            cs = slice(n * quarter, (n + 1) * quarter)
            upd[r, cs] = upd[r, cs] + along_x(1, r, n)

        def rn_send(j, c):
            d = g * per + lax.rem(me + j * 5, per)
            src = upd.at[pl.ds(pl.multiple_of(lax.div(d, 2) * 8, 8), 8), pl.ds(pl.multiple_of(lax.rem(d, 2) * half, half), half)]

            @pl.when(d != me)
            def _():
                remote(src, rnc.at[me], rn_s, rn_r.at[i], coords(d)).start()

            return c

        lax.fori_loop(0, per, rn_send, 0)
        pltpu.make_async_copy(upd.at[r], rn_h.at[r], local.at[11]).start()
        return c

    lax.fori_loop(0, parts, second, 0)
    rnc[me] = upd[my_rows, pl.ds(pl.multiple_of(lax.rem(me, 2) * half, half), half)]

    copies[7].wait()
    nb = rows // 8
    face[0:1, :] = jnp.zeros((1, cols), f32)
    face[pl.ds(nb, 8), :] = jnp.zeros((8, cols), f32)
    for f in range(1, nb):
        d_rn = upd[8 * f:8 * f + 1, :] - upd[8 * f - 1:8 * f, :]
        d_fs = fsv[8 * f:8 * f + 1, :] - fsv[8 * f - 1:8 * f, :]
        face[f:f + 1, :] = 0.5 * d_rn * d_fs
    tall = rows // steps
    eye = lax.broadcasted_iota(jnp.int32, (tall, 128), 0) == lax.broadcasted_iota(jnp.int32, (tall, 128), 1)
    row8 = lax.broadcasted_iota(jnp.int32, (8, cols), 0)

    for g in range(steps):
        r = slice(g * tall, (g + 1) * tall)
        d_rn = upd[r, half:half + 128] - pltpu.roll(upd[r, half - 128:half], 1, 1)
        d_fs = fsv[r, half:half + 128] - pltpu.roll(fsv[r, half - 128:half], 1, 1)
        px = 0.5 * d_rn * d_fs
        line = jnp.sum(jnp.where(eye, px[:, 0:1], 0.0), axis=0, keepdims=True)
        edge[g] = face[g * (tall // 8):g * (tall // 8) + 8, :]
        edge[g, 5:6, 0:128] = line

    def edge_send(i, c):
        g = lax.rem(tm + i, steps)
        remote(edge.at[g], edges.at[tm], ed_s, ed_r, (g, s)).start()
        return c

    lax.fori_loop(1, steps, edge_send, 0)
    edges[tm] = edge[tm]

    take(fsc.at[pl.ds(0, count - 1)], fs_r)
    own_fs.wait()
    lane8 = lax.broadcasted_iota(jnp.int32, (8, half), 1)
    sub8 = lax.broadcasted_iota(jnp.int32, (8, half), 0)

    sent(kbelow.at[pl.ds(0, 6 * width)], k2s)
    sent(kbelow, k3s)

    def cell(j):
        return (pl.ds(pl.multiple_of(lax.div(j, 2) * 8, 8), 8),
                pl.ds(pl.multiple_of(lax.rem(j, 2) * half, half), half))

    dx, dxm, dy, dym, dz = below, above, kbelow, kabove, fov

    def differences(j, c):
        w = cell(j)
        b = fsc[j]
        x = jnp.where(lane8 == half - 1, 0.0, pltpu.roll(b, half - 1, 1) - b)
        dx[w] = x
        dxm[w] = pltpu.roll(x, 1, 1)
        y = jnp.where(sub8 == 7, 0.0, pltpu.roll(b, 7, 0) - b)
        dy[w] = y
        dym[w] = pltpu.roll(y, 1, 0)
        dz[w] = jnp.where(lax.rem(j, layers) == layers - 1, 0.0, fsc[jnp.minimum(j + 1, count - 1)] - b)
        return c

    lax.fori_loop(0, count, differences, 0, unroll=2)
    zone = lax.div(tm, steps // parts)
    acc5[...] = jnp.zeros_like(acc5)

    def group(i, c):
        low = lax.rem(zone - i + parts, parts)

        @pl.when(low == lax.rem(tm, parts))
        def _():
            take(rnc.at[pl.ds(0, per - 1)], rn_r.at[i])

        @pl.when(low != lax.rem(tm, parts))
        def _():
            take(rnc.at[pl.ds(0, per)], rn_r.at[i])

        def layer(z, c):
            sums = [acc5[z, f] for f in range(5)]
            for k in range(steps // parts):
                j = (low + parts * k) * layers + z
                a, w = rnc[j], cell(j)
                up = rnc[jnp.where(z < layers - 1, j + 1, j)]
                terms = (a * dx[w], a * dxm[w], a * dy[w], a * dym[w], (up - a) * dz[w])
                sums = [p + q for p, q in zip(sums, terms)]
            for f in range(5):
                acc5[z, f] = sums[f]
            return c

        lax.fori_loop(0, layers, layer, 0)
        return c

    lax.fori_loop(0, parts, group, 0)
    fz = jnp.zeros((8, half), f32)
    for z in range(layers):
        sx, sxm, sy, sym, nz = [acc5[z, f] for f in range(5)]
        fx = (sxm - sx) + pltpu.roll(sxm, half - 1, 1) - pltpu.roll(sx, 1, 1)
        fy = (sym - sy) + pltpu.roll(sym, 7, 0) - pltpu.roll(sy, 1, 0)
        tot[z] = 0.5 * (fx + fy + fz + nz)
        fz = nz

    def tot_send(i, c):
        z = lax.rem(s + i, layers)
        remote(tot.at[z], got.at[s], gz_s, gz_r, (tm, z)).start()
        return c

    lax.fori_loop(1, layers, tot_send, 0)
    got[s] = tot[s]
    take(edges.at[pl.ds(0, steps - 1)], ed_r)
    total = edges[0]
    for t in range(1, steps):
        total = total + edges[t]
    face[0:8, :] = total
    column = jnp.sum(jnp.where(eye, face[5:6, 0:128], 0.0), axis=1, keepdims=True)
    take(got.at[pl.ds(0, layers - 1)], gz_r)
    for r in range(tall // 8):
        for h in range(2):
            cs = slice(h * half, (h + 1) * half)
            val = got[2 * r + h]
            val = val + jnp.where(sub8 == 0, face[r:r + 1, cs], 0.0)
            val = val + jnp.where(sub8 == 7, face[r + 1:r + 2, cs], 0.0)
            val = val + jnp.where(lane8 == (half - 1 if h == 0 else 0), column[8 * r:8 * r + 8], 0.0)
            grad[8 * r:8 * r + 8, cs] = val * (-1.0 / steps)
    out = pltpu.make_async_copy(grad, gr_h, local.at[12])
    out.start()

    @pl.when(not_last)
    def _():
        sent(kbelow.at[mine], k1s.at[0])
        for i in range(parts):
            sent(below.at[prows(i)], halo_s.at[0, i])

    @pl.when(not_first)
    def _():
        sent(kabove.at[mine], k1s.at[1])
        for i in range(parts):
            sent(above.at[prows(i)], halo_s.at[1, i])

    for p in range(2):
        sent(spec.at[p, pl.ds(0, count - 1)], fwd_s.at[p])
        sent(spec.at[p, pl.ds(0, count - 1)], bck_s.at[p])
    sent(fsc.at[pl.ds(0, count - 1)], fs_s)
    sent(rnc.at[pl.ds(0, count - 1)], rn_s)
    sent(edges.at[pl.ds(0, steps - 1)], ed_s)
    sent(got.at[pl.ds(0, layers - 1)], gz_s)
    take(upd, local.at[11])
    out.wait()


def body(forcing, iterate, forward_state, conductivity, terminal):
    rows, cols = iterate.shape[2:]
    steps, layers = lax.axis_size("tm"), lax.axis_size("space")
    count, half, quarter, part = steps * layers, cols // 2, cols // 4, rows // parts
    tx, ty = halves(table(cols)), halves(table(rows))
    ey = np.broadcast_to(eigen(rows)[:, None], (rows, quarter)).astype(np.float32)
    ex = np.broadcast_to(eigen(cols)[None, :], (8, cols)).astype(np.float32)
    tabs = np.zeros((6, cols, cols), ml_dtypes.bfloat16)
    tabs[0:2], tabs[2:4] = tx, tx.transpose(0, 2, 1)
    tabs[4:6, :rows, :rows], tabs[4:6, :rows, rows:2 * rows] = ty, ty.transpose(0, 2, 1)
    eigs = np.zeros((2 * cols, cols), np.float32)
    eigs[:rows, :quarter], eigs[rows:rows + 8] = ey, ex
    consts = [jnp.asarray(tabs), jnp.asarray(eigs)]
    V = pltpu.VMEM
    D = pltpu.SemaphoreType.DMA
    plane = V((rows, cols), f32)
    padded = V((rows + 16, cols), f32)
    scratch = [
        padded, padded, plane, plane, plane, plane, plane, plane,
        V((2, cols, cols), bf16), V((2, cols, cols), bf16), V((2, rows, rows), bf16), V((2, rows, rows), bf16),
        V((rows, quarter), f32), V((8, cols), f32),
        V((part, cols), bf16), V((part, cols), bf16), V((rows, cols), bf16), V((rows, cols), bf16),
        plane, V((2, count, 8, quarter), f32), plane,
        V((8, 128), bf16), V((8, 128), bf16), V((rows, half), bf16), V((rows, half), bf16),
        plane, V((count, 8, half), f32), V((count, 8, half), f32),
        V((rows // 8 + 8, cols), f32), V((steps, 8, cols), f32), V((steps, 8, cols), f32),
        V((layers, 8, half), f32), V((layers, 8, half), f32), V((rows // steps, cols), f32),
        V((layers, 5, 8, half), f32),
        D((14,)), D((2, parts)), D((2, parts)), D((2,)), D((2,)), D, D, D, D,
        D((2,)), D((2,)), D((2,)), D((2,)), D, D, D, D((parts,)), D, D, D, D,
    ]

    anywhere = pl.BlockSpec(memory_space=pl.ANY)
    rn, gr = pl.pallas_call(
        functools.partial(kernel, rows, cols, steps, layers),
        in_specs=[anywhere] * 7,
        out_specs=[anywhere] * 2,
        out_shape=[jax.ShapeDtypeStruct((rows, cols), f32), jax.ShapeDtypeStruct((rows // steps, cols), f32)],
        scratch_shapes=scratch,
        compiler_params=pltpu.CompilerParams(collective_id=0, has_side_effects=True, vmem_limit_bytes=52953088),
        name="correction",
    )(iterate[0, 0], forcing[0, 0], forward_state[0, 0], conductivity[0], terminal[0], *consts)
    return rn[None, None], gr[None]


def solution(mesh):
    field, layer = P("tm", "space", None, None), P("space", None, None)
    return jax.shard_map(
        body,
        mesh=mesh,
        in_specs=(field, field, field, layer, layer),
        out_specs=(field, P("space", "tm", None)),
        check_vma=False,
    )
```

```python
import functools
import math

import jax
import jax.numpy as jnp
import ml_dtypes
import numpy as np
from jax import lax
from jax.experimental import pallas as pl
from jax.experimental.pallas import tpu as pltpu
from jax.sharding import PartitionSpec as P

inv_dt = 4.0
wrap_alpha = 0.25
MESH = pl.DeviceIdType.MESH
stride = 37
parts = 4
FS1, FS2 = 24, 90
f32, bf16 = jnp.float32, jnp.bfloat16


def table(length):
    j = np.arange(length)[:, None]
    c = np.arange(length)[None, :]
    angle = math.pi * ((j * (2 * c + 1)) % (4 * length)) / (2 * length)
    factor = np.where(j == 0, math.sqrt(1.0 / length), math.sqrt(2.0 / length))
    return factor * np.cos(angle)


def eigen(length):
    return 2.0 - 2.0 * np.cos(math.pi * np.arange(length) / length)


def halves(tab):
    hi = tab.astype(ml_dtypes.bfloat16)
    lo = (tab - hi.astype(np.float64)).astype(ml_dtypes.bfloat16)
    return np.stack([hi, lo])


def split(x):
    hi = x.astype(bf16)
    return hi, (x - hi.astype(f32)).astype(bf16)


def dot3(ah, al, bh, bl):
    d = lambda a, b: jnp.dot(a, b, preferred_element_type=f32)
    return d(ah, bh) + d(ah, bl) + d(al, bh)


def take(ref, sem):
    pltpu.make_async_copy(ref, ref, sem).wait()


def kernel(rows, cols, steps, layers,
           it_h, fo_h, fs_h, ka_h, te_h, tab_h, eig_h,
           rn_h, gr_h,
           itv, kav, fov, fsv, below, above, kbelow, kabove,
           qx, qxt, qy, qyt, ey, ex,
           rh, rl, xh, xl, hat, spec, back, bh, bl, yh, yl, upd, fsc, rnc,
           face, edge, edges, tot, got, grad, acc5,
           local, halo_s, halo_r, k1s, k1r, k2s, k2r, k3s, k3r,
           fwd_s, fwd_r, bck_s, bck_r, fs_s, fs_r, rn_s, rn_r, ed_s, ed_r, gz_s, gz_r):
    tm, s = lax.axis_index("tm"), lax.axis_index("space")
    count = steps * layers
    me = tm * layers + s
    half, quarter = cols // 2, cols // 4
    part = rows // parts
    core, ypos, zhi = lax.rem(tm, 2), lax.rem(lax.div(tm, 2), 4), lax.div(tm, 8)

    def remote(src, dst, send, recv, to):
        return pltpu.make_async_remote_copy(src, dst, send, recv, device_id=to, device_id_type=MESH)

    def coords(d):
        return (lax.div(d, layers), lax.rem(d, layers))

    def sent(ref, sem):
        remote(ref, ref, sem, sem, (lax.rem(tm + 1, steps), s)).wait_send()

    qx_h, qxt_h = tab_h.at[0:2], tab_h.at[2:4]
    qy_h = tab_h.at[4:6, 0:rows, 0:rows]
    qyt_h = tab_h.at[4:6, 0:rows, rows:2 * rows]
    ey_h, ex_h = eig_h.at[0:rows, 0:quarter], eig_h.at[rows:rows + 8]
    body_it = itv.at[pl.ds(8, rows)]
    body_ka = kav.at[pl.ds(8, rows)]
    loads = [(it_h, body_it), (ka_h, body_ka), (fo_h, fov), (qxt_h, qxt), (qy_h, qy),
             (ey_h, ey), (ex_h, ex), (fs_h, fsv), (qx_h, qx), (qyt_h, qyt)]
    copies = [pltpu.make_async_copy(a, b, local.at[i]) for i, (a, b) in enumerate(loads)]
    for c in copies:
        c.start()

    barrier = pltpu.get_barrier_semaphore()

    others = [lax.rem(s + b, layers) for b in range(layers)]
    for b in range(1, layers):
        pl.semaphore_signal(barrier, 1, device_id=(tm, others[b]), device_id_type=MESH)

    def greet(a, c):
        to = lax.rem(tm + a, steps)
        for b in range(layers):
            pl.semaphore_signal(barrier, 1, device_id=(to, others[b]), device_id_type=MESH)
        return c

    lax.fori_loop(1, steps, greet, 0)
    pl.semaphore_wait(barrier, count - 1)

    width = rows // 8

    def krows(y, c):
        return pl.ds(pl.multiple_of((y * 2 + c) * width, 8), width)

    mine = krows(ypos, core)
    not_last, not_first = s < layers - 1, s > 0
    k_up = remote(ka_h.at[mine], kbelow.at[mine], k1s.at[0], k1r.at[0], (tm, jnp.minimum(s + 1, layers - 1)))
    k_dn = remote(ka_h.at[mine], kabove.at[mine], k1s.at[1], k1r.at[1], (tm, jnp.maximum(s - 1, 0)))

    @pl.when(not_last)
    def _():
        k_up.start()

    @pl.when(not_first)
    def _():
        k_dn.start()

    @pl.when(s == 0)
    def _():
        pltpu.make_async_copy(ka_h.at[mine], kbelow.at[mine], k1r.at[0]).start()

    @pl.when(s == layers - 1)
    def _():
        pltpu.make_async_copy(ka_h.at[mine], kabove.at[mine], k1r.at[1]).start()

    def prows(i):
        return pl.ds(pl.multiple_of(i * part, 8), part)

    def halo_start(i, c):
        r = prows(i)

        @pl.when(not_last)
        def _():
            remote(it_h.at[r], below.at[r], halo_s.at[0, i], halo_r.at[0, i], (tm, jnp.minimum(s + 1, layers - 1))).start()

        @pl.when(not_first)
        def _():
            remote(it_h.at[r], above.at[r], halo_s.at[1, i], halo_r.at[1, i], (tm, jnp.maximum(s - 1, 0))).start()

        @pl.when(s == 0)
        def _():
            pltpu.make_async_copy(it_h.at[r], below.at[r], halo_r.at[0, i]).start()

        @pl.when(s == layers - 1)
        def _():
            pltpu.make_async_copy(it_h.at[r], above.at[r], halo_r.at[1, i]).start()

        return c

    lax.fori_loop(0, parts, halo_start, 0)

    for i in range(3):
        copies[i].wait()
    last = jnp.where(tm == steps - 1, 1.0, 0.0).astype(f32)
    unit = 1.0 - last
    four = inv_dt * last

    @pl.when(tm == 0)
    def _():
        term = pltpu.make_async_copy(te_h, upd, local.at[13])
        term.start()
        term.wait()

        def opening(b, c):
            r = pl.ds(pl.multiple_of(b * 8, 8), 8)
            fov[r, :] = fov[r, :] + inv_dt * upd[r, :]
            return c

        lax.fori_loop(0, rows // 8, opening, 0)

    lane = lax.broadcasted_iota(jnp.int32, (8, cols), 1)
    sub = lax.broadcasted_iota(jnp.int32, (8, cols), 0)

    def in_plane(b, c):
        r = pl.multiple_of(b * 8, 8)
        vs, ks = itv[pl.ds(r, 24), :], kav[pl.ds(r, 24), :]
        v, vu, vd = vs[8:16], vs[9:17], vs[7:15]
        k, ku, kd = ks[8:16], ks[9:17], ks[7:15]
        fx = (0.5 * (pltpu.roll(k, cols - 1, 1) + k) - unit) * (pltpu.roll(v, cols - 1, 1) - v)
        fx = jnp.where(lane == cols - 1, 0.0, fx)
        fu = jnp.where(sub + r == rows - 1, 0.0, (0.5 * (ku + k) - unit) * (vu - v))
        fd = jnp.where(sub + r == 0, 0.0, (0.5 * (k + kd) - unit) * (v - vd))
        applied = (pltpu.roll(fx, 1, 1) - fx) + (fd - fu)
        fov[pl.ds(r, 8), :] = fov[pl.ds(r, 8), :] - (four * v + applied)
        return c

    blocks = rows // 8
    lax.fori_loop(0, blocks // 4, in_plane, 0)
    take(kbelow.at[mine], k1r.at[0])
    take(kabove.at[mine], k1r.at[1])

    def along_y(i, c):
        to = (zhi * 8 + lax.rem(ypos + i, 4) * 2 + core, s)
        remote(kbelow.at[mine], kbelow.at[mine], k2s, k2r, to).start()
        remote(kabove.at[mine], kabove.at[mine], k2s, k2r, to).start()
        return c

    lax.fori_loop(1, 4, along_y, 0)
    lax.fori_loop(blocks // 4, blocks, in_plane, 0)
    take(kbelow.at[pl.ds(0, 6 * width)], k2r)

    def across(i, c):
        r = krows(i, core)
        to = (zhi * 8 + ypos * 2 + 1 - core, s)
        remote(kbelow.at[r], kbelow.at[r], k3s, k3r, to).start()
        remote(kabove.at[r], kabove.at[r], k3s, k3r, to).start()
        return c

    lax.fori_loop(0, 4, across, 0)
    take(kbelow, k3r)
    copies[3].wait()

    def fs_send(i, c):
        d = lax.rem(me + i * stride, count)
        src = fs_h.at[pl.ds(pl.multiple_of(lax.div(d, 2) * 8, 8), 8), pl.ds(pl.multiple_of(lax.rem(d, 2) * half, half), half)]
        remote(src, fsc.at[me], fs_s, fs_r, coords(d)).start()
        return c

    def arrive(i, c):
        r = prows(i)
        take(below.at[r], halo_r.at[0, i])
        take(above.at[r], halo_r.at[1, i])

        def resid(b, c):
            q = pl.multiple_of(i * part + b * 16, 16)
            at = lambda ref, off=0: ref[pl.ds(q + off, 16), :]
            v, k = at(itv, 8), at(kav, 8)
            x = at(fov) - (0.5 * (k + at(kbelow)) - unit) * (v - at(below))
            x = x - (0.5 * (k + at(kabove)) - unit) * (v - at(above))
            hi, lo = split(x)
            o = pl.multiple_of(b * 16, 16)
            rh[pl.ds(o, 16), :] = hi
            rl[pl.ds(o, 16), :] = lo
            return c

        lax.fori_loop(0, part // 16, resid, 0)
        for n in range(4):
            cs = slice(n * quarter, (n + 1) * quarter)
            acc = dot3(rh[...], rl[...], qxt[0, :, cs], qxt[1, :, cs])
            hi, lo = split(acc)
            xh[pl.ds(pl.multiple_of(i * part, 16), part), cs] = hi
            xl[pl.ds(pl.multiple_of(i * part, 16), part), cs] = lo
        return c

    lax.fori_loop(1, FS1, fs_send, 0)
    lax.fori_loop(0, parts, arrive, 0)
    copies[4].wait()

    my_rows = pl.ds(pl.multiple_of(lax.div(me, 2) * 8, 8), 8)

    def piece(d, p):
        return (pl.ds(pl.multiple_of(lax.div(d, 2) * 8, 8), 8),
                pl.ds(pl.multiple_of(p * half + lax.rem(d, 2) * quarter, quarter), quarter))

    for p in range(2):
        for n in range(2):
            cs = slice(p * half + n * quarter, p * half + (n + 1) * quarter)
            hat[:, cs] = dot3(qy[0], qy[1], xh[:, cs], xl[:, cs])

        def fwd(i, c, p=p):
            d = lax.rem(me + i * stride, count)
            remote(hat.at[piece(d, p)], spec.at[p, me], fwd_s.at[p], fwd_r.at[p], coords(d)).start()
            return c

        lax.fori_loop(1, count, fwd, 0)
        spec[p, me] = hat[piece(me, p)]

    lax.fori_loop(FS1, FS2, fs_send, 0)
    own_fs = pltpu.make_async_copy(fs_h.at[my_rows, pl.ds(pl.multiple_of(lax.rem(me, 2) * half, half), half)], fsc.at[me], local.at[10])
    own_fs.start()

    copies[5].wait()
    copies[6].wait()
    tab = table(layers)
    lam = eigen(layers)
    lz = layers // 2
    for p in range(2):
        take(spec.at[p, pl.ds(0, count - 1)], fwd_r.at[p])
        mu = ey[my_rows, :] + ex[:, pl.ds(pl.multiple_of(p * half + lax.rem(me, 2) * quarter, quarter), quarter)]
        w = [1.0 / (mu + (inv_dt + float(lam[j]))) for j in range(layers)]
        q = [inv_dt * w[j] for j in range(layers)]

        def forward(m, state, p=p, w=w, q=q):
            v = [spec[p, m * layers + z] for z in range(layers)]
            even = [v[z] + v[layers - 1 - z] for z in range(lz)]
            odd = [v[z] - v[layers - 1 - z] for z in range(lz)]
            new = []
            for j in range(layers):
                src = odd if j % 2 else even
                acc = src[0] * float(tab[j, 0])
                for z in range(1, lz):
                    acc = acc + src[z] * float(tab[j, z])
                u = q[j] * state[j] + w[j] * acc
                spec[p, m * layers + j] = u
                new.append(u)
            return tuple(new)

        state = lax.fori_loop(0, steps, forward, tuple(jnp.zeros((8, quarter), f32) for _ in range(layers)))
        carry = []
        for j in range(layers):
            t = q[j]
            for _ in range(int(math.log2(steps))):
                t = t * t
            carry.append(wrap_alpha * state[j] / (1.0 - wrap_alpha * t))

        def backward(m, carry, p=p, q=q):
            carry = tuple(q[j] * carry[j] for j in range(layers))
            u = [spec[p, m * layers + j] + carry[j] for j in range(layers)]
            for z in range(lz):
                e = u[0] * float(tab[0, z])
                o = u[1] * float(tab[1, z])
                for j in range(2, layers, 2):
                    e = e + u[j] * float(tab[j, z])
                    o = o + u[j + 1] * float(tab[j + 1, z])
                spec[p, m * layers + z] = e + o
                spec[p, m * layers + layers - 1 - z] = e - o
            return carry

        lax.fori_loop(0, steps, backward, tuple(carry))

        def bck(i, c, p=p):
            d = lax.rem(me + i * stride, count)
            remote(spec.at[p, d], back.at[piece(me, p)], bck_s.at[p], bck_r.at[p], coords(d)).start()
            return c

        lax.fori_loop(1, count, bck, 0)
        back[piece(me, p)] = spec[p, me]

    lax.fori_loop(FS2, count, fs_send, 0)
    copies[8].wait()
    copies[9].wait()

    def to_plane(p):
        take(spec.at[p, pl.ds(0, count - 1)], bck_r.at[p])
        for n in range(2):
            cs = slice(p * half + n * quarter, p * half + (n + 1) * quarter)
            hi, lo = split(back[:, cs])
            acc = dot3(qyt[0], qyt[1], hi, lo)
            hi, lo = split(acc)
            yh[:, n * quarter:(n + 1) * quarter] = hi
            yl[:, n * quarter:(n + 1) * quarter] = lo

    def along_x(p, r, n):
        cs = slice(n * quarter, (n + 1) * quarter)
        ks = slice(p * half, (p + 1) * half)
        return dot3(yh[r, :], yl[r, :], qx[0, ks, cs], qx[1, ks, cs])

    to_plane(0)

    def first(i, c):
        r = pl.ds(pl.multiple_of(i * part, 16), part)
        for n in range(4):
            cs = slice(n * quarter, (n + 1) * quarter)
            upd[r, cs] = last * itv[pl.ds(pl.multiple_of(i * part, 16) + 8, part), cs] + along_x(0, r, n)
        return c

    lax.fori_loop(0, parts, first, 0)
    to_plane(1)
    per = count // parts

    def second(i, c):
        g = lax.rem(i + tm, parts)
        start = pl.multiple_of(g * part, 16)
        r = pl.ds(start, part)
        for n in range(4):
            cs = slice(n * quarter, (n + 1) * quarter)
            upd[r, cs] = upd[r, cs] + along_x(1, r, n)

        def rn_send(j, c):
            d = g * per + lax.rem(me + j * 5, per)
            src = upd.at[pl.ds(pl.multiple_of(lax.div(d, 2) * 8, 8), 8), pl.ds(pl.multiple_of(lax.rem(d, 2) * half, half), half)]

            @pl.when(d != me)
            def _():
                remote(src, rnc.at[me], rn_s, rn_r.at[i], coords(d)).start()

            return c

        lax.fori_loop(0, per, rn_send, 0)
        pltpu.make_async_copy(upd.at[r], rn_h.at[r], local.at[11]).start()
        return c

    lax.fori_loop(0, parts, second, 0)
    rnc[me] = upd[my_rows, pl.ds(pl.multiple_of(lax.rem(me, 2) * half, half), half)]

    copies[7].wait()
    nb = rows // 8
    face[0:1, :] = jnp.zeros((1, cols), f32)
    face[pl.ds(nb, 8), :] = jnp.zeros((8, cols), f32)
    for f in range(1, nb):
        d_rn = upd[8 * f:8 * f + 1, :] - upd[8 * f - 1:8 * f, :]
        d_fs = fsv[8 * f:8 * f + 1, :] - fsv[8 * f - 1:8 * f, :]
        face[f:f + 1, :] = 0.5 * d_rn * d_fs
    tall = rows // steps
    eye = lax.broadcasted_iota(jnp.int32, (tall, 128), 0) == lax.broadcasted_iota(jnp.int32, (tall, 128), 1)
    row8 = lax.broadcasted_iota(jnp.int32, (8, cols), 0)

    for g in range(steps):
        r = slice(g * tall, (g + 1) * tall)
        d_rn = upd[r, half:half + 128] - pltpu.roll(upd[r, half - 128:half], 1, 1)
        d_fs = fsv[r, half:half + 128] - pltpu.roll(fsv[r, half - 128:half], 1, 1)
        px = 0.5 * d_rn * d_fs
        line = jnp.sum(jnp.where(eye, px[:, 0:1], 0.0), axis=0, keepdims=True)
        edge[g] = face[g * (tall // 8):g * (tall // 8) + 8, :]
        edge[g, 5:6, 0:128] = line

    def edge_send(i, c):
        g = lax.rem(tm + i, steps)
        remote(edge.at[g], edges.at[tm], ed_s, ed_r, (g, s)).start()
        return c

    lax.fori_loop(1, steps, edge_send, 0)
    edges[tm] = edge[tm]

    take(fsc.at[pl.ds(0, count - 1)], fs_r)
    own_fs.wait()
    lane8 = lax.broadcasted_iota(jnp.int32, (8, half), 1)
    sub8 = lax.broadcasted_iota(jnp.int32, (8, half), 0)

    sent(kbelow.at[pl.ds(0, 6 * width)], k2s)
    sent(kbelow, k3s)

    def cell(j):
        return (pl.ds(pl.multiple_of(lax.div(j, 2) * 8, 8), 8),
                pl.ds(pl.multiple_of(lax.rem(j, 2) * half, half), half))

    dx, dxm, dy, dym, dz = below, above, kbelow, kabove, fov

    def differences(j, c):
        w = cell(j)
        b = fsc[j]
        x = jnp.where(lane8 == half - 1, 0.0, pltpu.roll(b, half - 1, 1) - b)
        dx[w] = x
        dxm[w] = pltpu.roll(x, 1, 1)
        y = jnp.where(sub8 == 7, 0.0, pltpu.roll(b, 7, 0) - b)
        dy[w] = y
        dym[w] = pltpu.roll(y, 1, 0)
        dz[w] = jnp.where(lax.rem(j, layers) == layers - 1, 0.0, fsc[jnp.minimum(j + 1, count - 1)] - b)
        return c

    lax.fori_loop(0, count, differences, 0, unroll=2)
    zone = lax.div(tm, steps // parts)
    acc5[...] = jnp.zeros_like(acc5)

    def group(i, c):
        low = lax.rem(zone - i + parts, parts)

        @pl.when(low == lax.rem(tm, parts))
        def _():
            take(rnc.at[pl.ds(0, per - 1)], rn_r.at[i])

        @pl.when(low != lax.rem(tm, parts))
        def _():
            take(rnc.at[pl.ds(0, per)], rn_r.at[i])

        def layer(z, c):
            sums = [acc5[z, f] for f in range(5)]
            for k in range(steps // parts):
                j = (low + parts * k) * layers + z
                a, w = rnc[j], cell(j)
                up = rnc[jnp.where(z < layers - 1, j + 1, j)]
                terms = (a * dx[w], a * dxm[w], a * dy[w], a * dym[w], (up - a) * dz[w])
                sums = [p + q for p, q in zip(sums, terms)]
            for f in range(5):
                acc5[z, f] = sums[f]
            return c

        lax.fori_loop(0, layers, layer, 0)
        return c

    lax.fori_loop(0, parts, group, 0)
    fz = jnp.zeros((8, half), f32)
    for z in range(layers):
        sx, sxm, sy, sym, nz = [acc5[z, f] for f in range(5)]
        fx = (sxm - sx) + pltpu.roll(sxm, half - 1, 1) - pltpu.roll(sx, 1, 1)
        fy = (sym - sy) + pltpu.roll(sym, 7, 0) - pltpu.roll(sy, 1, 0)
        tot[z] = 0.5 * (fx + fy + fz + nz)
        fz = nz

    def tot_send(i, c):
        z = lax.rem(s + i, layers)
        remote(tot.at[z], got.at[s], gz_s, gz_r, (tm, z)).start()
        return c

    lax.fori_loop(1, layers, tot_send, 0)
    got[s] = tot[s]
    take(edges.at[pl.ds(0, steps - 1)], ed_r)
    total = edges[0]
    for t in range(1, steps):
        total = total + edges[t]
    face[0:8, :] = total
    column = jnp.sum(jnp.where(eye, face[5:6, 0:128], 0.0), axis=1, keepdims=True)
    take(got.at[pl.ds(0, layers - 1)], gz_r)
    for r in range(tall // 8):
        for h in range(2):
            cs = slice(h * half, (h + 1) * half)
            val = got[2 * r + h]
            val = val + jnp.where(sub8 == 0, face[r:r + 1, cs], 0.0)
            val = val + jnp.where(sub8 == 7, face[r + 1:r + 2, cs], 0.0)
            val = val + jnp.where(lane8 == (half - 1 if h == 0 else 0), column[8 * r:8 * r + 8], 0.0)
            grad[8 * r:8 * r + 8, cs] = val * (-1.0 / steps)
    out = pltpu.make_async_copy(grad, gr_h, local.at[12])
    out.start()

    @pl.when(not_last)
    def _():
        sent(kbelow.at[mine], k1s.at[0])
        for i in range(parts):
            sent(below.at[prows(i)], halo_s.at[0, i])

    @pl.when(not_first)
    def _():
        sent(kabove.at[mine], k1s.at[1])
        for i in range(parts):
            sent(above.at[prows(i)], halo_s.at[1, i])

    for p in range(2):
        sent(spec.at[p, pl.ds(0, count - 1)], fwd_s.at[p])
        sent(spec.at[p, pl.ds(0, count - 1)], bck_s.at[p])
    sent(fsc.at[pl.ds(0, count - 1)], fs_s)
    sent(rnc.at[pl.ds(0, count - 1)], rn_s)
    sent(edges.at[pl.ds(0, steps - 1)], ed_s)
    sent(got.at[pl.ds(0, layers - 1)], gz_s)
    take(upd, local.at[11])
    out.wait()


def body(forcing, iterate, forward_state, conductivity, terminal):
    rows, cols = iterate.shape[2:]
    steps, layers = lax.axis_size("tm"), lax.axis_size("space")
    count, half, quarter, part = steps * layers, cols // 2, cols // 4, rows // parts
    tx, ty = halves(table(cols)), halves(table(rows))
    ey = np.broadcast_to(eigen(rows)[:, None], (rows, quarter)).astype(np.float32)
    ex = np.broadcast_to(eigen(cols)[None, :], (8, cols)).astype(np.float32)
    tabs = np.zeros((6, cols, cols), ml_dtypes.bfloat16)
    tabs[0:2], tabs[2:4] = tx, tx.transpose(0, 2, 1)
    tabs[4:6, :rows, :rows], tabs[4:6, :rows, rows:2 * rows] = ty, ty.transpose(0, 2, 1)
    eigs = np.zeros((2 * cols, cols), np.float32)
    eigs[:rows, :quarter], eigs[rows:rows + 8] = ey, ex
    consts = [jnp.asarray(tabs), jnp.asarray(eigs)]
    V = pltpu.VMEM
    D = pltpu.SemaphoreType.DMA
    plane = V((rows, cols), f32)
    padded = V((rows + 16, cols), f32)
    scratch = [
        padded, padded, plane, plane, plane, plane, plane, plane,
        V((2, cols, cols), bf16), V((2, cols, cols), bf16), V((2, rows, rows), bf16), V((2, rows, rows), bf16),
        V((rows, quarter), f32), V((8, cols), f32),
        V((part, cols), bf16), V((part, cols), bf16), V((rows, cols), bf16), V((rows, cols), bf16),
        plane, V((2, count, 8, quarter), f32), plane,
        V((8, 128), bf16), V((8, 128), bf16), V((rows, half), bf16), V((rows, half), bf16),
        plane, V((count, 8, half), f32), V((count, 8, half), f32),
        V((rows // 8 + 8, cols), f32), V((steps, 8, cols), f32), V((steps, 8, cols), f32),
        V((layers, 8, half), f32), V((layers, 8, half), f32), V((rows // steps, cols), f32),
        V((layers, 5, 8, half), f32),
        D((14,)), D((2, parts)), D((2, parts)), D((2,)), D((2,)), D, D, D, D,
        D((2,)), D((2,)), D((2,)), D((2,)), D, D, D, D((parts,)), D, D, D, D,
    ]

    anywhere = pl.BlockSpec(memory_space=pl.ANY)
    rn, gr = pl.pallas_call(
        functools.partial(kernel, rows, cols, steps, layers),
        in_specs=[anywhere] * 7,
        out_specs=[anywhere] * 2,
        out_shape=[jax.ShapeDtypeStruct((rows, cols), f32), jax.ShapeDtypeStruct((rows // steps, cols), f32)],
        scratch_shapes=scratch,
        compiler_params=pltpu.CompilerParams(collective_id=0, has_side_effects=True, vmem_limit_bytes=52953088),
        name="correction",
    )(iterate[0, 0], forcing[0, 0], forward_state[0, 0], conductivity[0], terminal[0], *consts)
    return rn[None, None], gr[None]


def solution(mesh):
    field, layer = P("tm", "space", None, None), P("space", None, None)
    return jax.shard_map(
        body,
        mesh=mesh,
        in_specs=(field, field, field, layer, layer),
        out_specs=(field, P("space", "tm", None)),
        check_vma=False,
    )
```
